32 devices in a mesh: ocean: 2 (over core), ice: 16 (over z, y, x).
Axes of the slice: x: 2, y: 2, z: 4, core: 2. Of those that a mesh axis runs over, the one named last changes fastest.
Arguments:
- velocity: float32 [128, 128, 128], P('ocean', 'ice'), may hold values from -6 to 6
- stress: float32 [128, 128, 128], P('ocean', 'ice'), may hold values from -6 to 6
- thickness: float32 [128, 128, 128], P('ocean', 'ice'), may hold values from 0.5 to 2
- forcing: float32 [128, 128, 128], P('ocean', 'ice'), may hold values from -6 to 6
- switch: int32 [128, 128, 128], P('ocean', 'ice'), may hold values 0 or 1
- covered: int32 [128], P('ocean'), may hold values from 0 to 1, as said below
- reinit: int32 [128], P('ocean'), may hold values 0 or 1
- cot_velocity: float32 [128, 128, 128], P('ocean', 'ice'), may hold values from -6 to 6
- cot_stress: float32 [128, 128, 128], P('ocean', 'ice'), may hold values from -6 to 6
- kernel: float32 [128, 128], replicated, may hold values from 0 to 1, as said below
Outputs:
- grad_velocity: float32 [128, 128, 128], P('ocean', 'ice')
- grad_stress: float32 [128, 128, 128], P('ocean', 'ice')
- grad_thickness: float32 [128, 128, 128], P('ocean', 'ice')
- grad_forcing: float32 [128, 128, 128], P('ocean', 'ice')
The draws below stay inside these ranges and needn't reach their ends.
Inputs may be any that keep to these rules, and one draw needn't show every extreme that they name: Exactly 32 blocks are covered; one index of ocean holds 31 of them and the other holds one. The kernel's diagonal exceeds the sum of each row's other entries.
All inputs are finite; a program needn't handle non-finite values. No bound on the sum of `switch` or of `reinit` on one device may be relied on, other than what follows from the above.
Results may differ from the reference program's by a relative error of at most 0.00015.
Values sent between devices are 32-bit elements; how exact they have to be, the bound alone decides.
A program may use at most 64 MiB of HBM per device.

```python
import jax
import jax.numpy as jnp
from jax import lax

CELLS = 128
BLOCKS_DEV = 64
SUB = 8
WINDOWS = 2
ROWS = 128
BLOCKS = 128


def draw_covered(key, part):
    groups = BLOCKS // BLOCKS_DEV
    heavy = jax.random.randint(jax.random.fold_in(key, 11), (), 0, groups)
    pieces = []
    for group in range(groups):
        order = jax.random.permutation(jax.random.fold_in(key, 20 + group), BLOCKS_DEV)
        wanted = jnp.where(heavy == group, BLOCKS_DEV // 2 - 1, 1)
        pieces.append((order < wanted).astype(jnp.int32))
    return jnp.concatenate(pieces)


def draw_kernel(key, part):
    inner = jax.random.fold_in(key, 21)
    spread = jax.random.uniform(inner, (ROWS, ROWS), jnp.float32, 0.0, 0.8)
    return spread / ROWS + 0.6 * jnp.eye(ROWS, dtype=jnp.float32)


def set_ends(values, key, low, largest):
    index_at = [jax.random.randint(jax.random.fold_in(key, axis), (), 0, length) for axis, length in enumerate(values.shape)]
    longest = values.shape.index(max(values.shape))
    neighbour = index_at[:longest] + [(index_at[longest] + 1) % values.shape[longest]] + index_at[longest + 1:]
    return values.at[tuple(index_at)].set(low).at[tuple(neighbour)].set(largest)


def block_levels(stream_key, shape, shards, low, largest):
    def one(position, blocks):
        heights = jax.random.uniform(jax.random.fold_in(jax.random.fold_in(stream_key, 6), position), (blocks,), jnp.float32, low / len(shards), largest / len(shards))
        return jnp.repeat(jnp.exp(heights), shape[position] // blocks).reshape((-1,) + (1,) * (len(shape) - position - 1))

    gain = one(*shards[0])
    for cut in shards[1:]:
        gain = gain * one(*cut)
    return gain


def noise(rng, dims, deviation, reach, cuts=(), kind=jnp.bfloat16):
    array = jax.random.normal(rng, dims, jnp.float32) * deviation
    if len(cuts) > 0:
        array = block_levels(rng, dims, cuts, -0.22, 0.18) * array
    return jnp.clip(array, min=-reach, max=reach).astype(kind)


def setup_inputs(seed: int = 0) -> dict:
    key_of = jax.random.split(jax.random.key(seed), 11)
    velocity = noise(key_of[0], (BLOCKS, ROWS, CELLS), 1.0, 6.0, ((0, 2), (1, 16)), jnp.float32)
    stress = noise(key_of[1], (BLOCKS, ROWS, CELLS), 1.0, 6.0, ((0, 2), (1, 16)), jnp.float32)
    thickness = jnp.clip(0.5 + 1.5 * jax.random.uniform(key_of[2], (BLOCKS, ROWS, CELLS), jnp.float32) ** block_levels(key_of[2], (BLOCKS, ROWS, CELLS), ((0, 2), (1, 16)), -0.2, 0.2), 0.5, 2.0)
    forcing = noise(key_of[3], (BLOCKS, ROWS, CELLS), 1.0, 6.0, ((0, 2), (1, 16)), jnp.float32)
    switch = set_ends((jax.random.randint(key_of[4], (BLOCKS, ROWS, CELLS), 0, 2) < 1).astype(jnp.int32), jax.random.fold_in(key_of[4], 1), 0, 1)
    covered = draw_covered(jax.random.fold_in(key_of[10], 71), 0)
    reinit = set_ends((jax.random.randint(key_of[6], (BLOCKS,), 0, 2) < 1).astype(jnp.int32), jax.random.fold_in(key_of[6], 1), 0, 1)
    cot_velocity = noise(key_of[7], (BLOCKS, ROWS, CELLS), 1.0, 6.0, ((0, 2), (1, 16)), jnp.float32)
    cot_stress = noise(key_of[8], (BLOCKS, ROWS, CELLS), 1.0, 6.0, ((0, 2), (1, 16)), jnp.float32)
    kernel = draw_kernel(jax.random.fold_in(key_of[10], 71), 0)
    return dict(velocity=velocity, stress=stress, thickness=thickness, forcing=forcing, switch=switch, covered=covered, reinit=reinit, cot_velocity=cot_velocity, cot_stress=cot_stress, kernel=kernel)


PLASTIC = 0.25
VISCOUS = 1.0
GAMMA = 0.6
BETA = 0.9
STEP = 0.04

def forward_diff(x):
    upper = jnp.pad(x, ((0, 0), (1, 0), (0, 0)))[:, :-1]
    left = jnp.pad(x, ((0, 0), (0, 0), (1, 0)))[:, :, :-1]
    return 2.0 * x - upper - left

def backward_diff(x):
    lower = jnp.pad(x, ((0, 0), (0, 1), (0, 0)))[:, 1:]
    right = jnp.pad(x, ((0, 0), (0, 0), (0, 1)))[:, :, 1:]
    return 2.0 * x - lower - right

def evolve(velo, stress_now, source, force, keep, kernel):
    zeta = jnp.einsum('ij,bjc->bic', kernel, source, precision=lax.Precision.HIGHEST)
    u_now, s_now = (velo, stress_now)
    for window in range(WINDOWS):
        if window > 0:
            s_now = s_now * keep[:, None, None]
        for step in range(SUB):
            s_now = GAMMA * s_now + zeta * forward_diff(u_now)
            u_now = BETA * u_now - STEP * backward_diff(s_now) + STEP * force
    return (u_now, s_now)

def one_group(items):
    velo, stress_now, source, force, keep, kernel, cot_u, cot_s = items
    outputs, pullback = jax.vjp(lambda a, b, c, d: evolve(a, b, c, d, keep, kernel), velo, stress_now, source, force)
    return pullback((cot_u, cot_s))

def reference(velocity, stress, thickness, forcing, switch, covered, reinit, cot_velocity, cot_stress, kernel):
    coef = jnp.where(switch == 1, PLASTIC, VISCOUS).astype(jnp.float32)
    source = thickness * coef
    keep = (1 - reinit).astype(jnp.float32)
    groups = BLOCKS // BLOCKS_DEV

    def split(x):
        return x.reshape((groups, BLOCKS_DEV) + x.shape[1:])

    def mapped(items):
        velo, stress_now, src, force, kp, cot_u, cot_s = items
        return one_group((velo, stress_now, src, force, kp, kernel, cot_u, cot_s))
    gu, gs, gq, gf = lax.map(mapped, (split(velocity), split(stress), split(source), split(forcing), split(keep), split(cot_velocity), split(cot_stress)))
    live = covered.astype(jnp.float32)[:, None, None]
    shape = velocity.shape
    gu = gu.reshape(shape) * live
    gs = gs.reshape(shape) * live
    gq = gq.reshape(shape) * live
    gf = gf.reshape(shape) * live
    return (gu, gs, gq * coef, gf)
```

```python
import functools

import jax
import jax.numpy as jnp
from jax import lax
from jax.experimental import pallas as pl
from jax.experimental.pallas import tpu as pltpu
from jax.sharding import PartitionSpec as P

SUB = 8
WINDOWS = 2
COVERED = 32

PLASTIC = 0.25
VISCOUS = 1.0
GAMMA = 0.6
BETA = 0.9
STEP = 0.04

MESH = pl.DeviceIdType.MESH
FIELDS = 6
PHASES = ((0, 1), (1, 3), (3, 6))
GRADS = 4
BACK = ((0, 3), (3, 4))


def plan_kernel(work, covered, reinit, idx, keep, home, heavy):
    blocks = covered.shape[0]

    def clear(k, unused):
        idx[k] = 0
        keep[k] = 0
        return unused

    lax.fori_loop(0, idx.shape[0], clear, 0)

    def one(b, rank):
        place = jnp.minimum(rank, idx.shape[0] - 1)
        idx[place] = b
        keep[place] = 1 - reinit[b]
        home[b] = place
        return rank + covered[b]

    count = lax.fori_loop(0, blocks, one, 0)
    many = jnp.where(count > work, 1, 0)
    heavy[0] = many

    def fix(b, unused):
        home[b] = jnp.where(many == 1, home[b], work - 1)
        return unused

    lax.fori_loop(0, blocks, fix, 0)


def forward_diff(x, row, col):
    upper = jnp.where(row == 0, 0.0, pltpu.roll(x, 1, 0))
    left = jnp.where(col == 0, 0.0, pltpu.roll(x, 1, 1))
    return 2.0 * x - upper - left


def backward_diff(x, row, col):
    rows, cells = x.shape
    lower = jnp.where(row == rows - 1, 0.0, pltpu.roll(x, rows - 1, 0))
    right = jnp.where(col == cells - 1, 0.0, pltpu.roll(x, cells - 1, 1))
    return 2.0 * x - lower - right


def work_kernel(
    n, work, idx, keep, heavy, velo, stress, thick, force, switch, cot_u, cot_s, kernel, ret,
    own, over, got, keep_own, keep_over, keep_got, send, fields, zeta, total, grads,
    ex_send, ex_recv, go_send, go_recv, back_send, back_recv, fwd_send, fwd_recv,
):
    ocean = lax.axis_index("ocean")
    me = lax.axis_index("ice")
    other = 1 - ocean
    stride = n // work
    rows_dev = velo.shape[1]
    cells = velo.shape[2]
    rows = kernel.shape[0]
    my_slot = me // stride
    is_owner = me % stride == 0

    def when_owner(body):
        if stride == 1:
            body()
        else:
            pl.when(is_owner)(body)

    barrier = pltpu.get_barrier_semaphore()

    def greet(d, unused):
        pl.semaphore_signal(
            barrier, inc=1, device_id=(ocean, lax.rem(me + d, n)), device_id_type=MESH
        )
        return unused

    pl.semaphore_signal(barrier, inc=1, device_id=(other, me), device_id_type=MESH)
    lax.fori_loop(1, n, greet, 0)

    def pack(dst, keep_dst, k, rank):
        b = idx[rank]
        coef = jnp.where(switch[b] == 1, PLASTIC, VISCOUS)
        dst[0, k] = thick[b] * coef
        dst[1, k] = cot_u[b]
        dst[2, k] = cot_s[b]
        dst[3, k] = velo[b]
        dst[4, k] = stress[b]
        dst[5, k] = force[b]
        keep_dst[k] = jnp.full((rows_dev, cells), keep[rank].astype(jnp.float32))

    for k in range(work - 1):
        pack(over, keep_over, k, work + k)

    pl.semaphore_wait(barrier, n)

    def exchange(p):
        if p == len(PHASES):
            src, dst = keep_over, keep_got
        else:
            lo, hi = PHASES[p]
            src, dst = over.at[lo:hi], got.at[lo:hi]
        return pltpu.make_async_remote_copy(
            src_ref=src, dst_ref=dst, send_sem=ex_send.at[p], recv_sem=ex_recv.at[p],
            device_id=(other, me), device_id_type=MESH,
        )

    for p in range(len(PHASES) + 1):
        exchange(p).start()
    for k in range(work):
        pack(own, keep_own, k, k)

    full = jnp.full((rows_dev, cells), heavy[0]) == 1
    my_rows = pl.ds(pl.multiple_of(me * rows_dev, rows_dev), rows_dev)

    def go(p, slot, target):
        lo, hi = PHASES[p]
        return pltpu.make_async_remote_copy(
            src_ref=send.at[slot, lo:hi], dst_ref=fields.at[lo:hi, my_rows, :],
            send_sem=go_send.at[p, slot], recv_sem=go_recv.at[p, me],
            device_id=(ocean, target), device_id_type=MESH,
        )

    def arrive(p, j):
        lo, hi = PHASES[p]
        there = pl.ds(pl.multiple_of(j * rows_dev, rows_dev), rows_dev)
        return pltpu.make_async_remote_copy(
            src_ref=send.at[0, lo:hi], dst_ref=fields.at[lo:hi, there, :],
            send_sem=go_send.at[p, 0], recv_sem=go_recv.at[p, j],
            device_id=(ocean, j), device_id_type=MESH,
        )

    for p, (lo, hi) in enumerate(PHASES):
        exchange(p).wait_recv()
        for k in range(work):
            for f in range(lo, hi):
                rest = got[f, k] if k < work - 1 else own[f, 0]
                send[k, f] = jnp.where(full, own[f, k], rest)

        def start(d, unused, p=p):
            slot = lax.rem(my_slot + d, work)
            go(p, slot, slot * stride).start()
            return unused

        lax.fori_loop(1, work, start, 0)

        def local(lo=lo, hi=hi):
            fields[lo:hi, my_rows, :] = send[my_slot, lo:hi]

        when_owner(local)
        if stride > 1:
            pl.when(jnp.logical_not(is_owner))(lambda p=p: go(p, my_slot, my_slot * stride).start())
    exchange(len(PHASES)).wait_recv()

    def wait_phase(p):
        def one(d, unused):
            arrive(p, lax.rem(me + n - d, n)).wait_recv()
            return unused

        lax.fori_loop(1, n, one, 0)

    def back(p, j):
        lo, hi = BACK[p]
        there = pl.ds(pl.multiple_of(j * rows_dev, rows_dev), rows_dev)
        return pltpu.make_async_remote_copy(
            src_ref=grads.at[lo:hi, there, :], dst_ref=ret.at[lo:hi, my_slot],
            send_sem=back_send.at[p, j], recv_sem=back_recv.at[p, my_slot],
            device_id=(ocean, j), device_id_type=MESH,
        )

    def back_arrive(p, slot):
        lo, hi = BACK[p]
        return pltpu.make_async_remote_copy(
            src_ref=grads.at[lo:hi, my_rows, :], dst_ref=ret.at[lo:hi, slot],
            send_sem=back_send.at[p, 0], recv_sem=back_recv.at[p, slot],
            device_id=(ocean, slot * stride), device_id_type=MESH,
        )

    def send_back(p):
        lo, hi = BACK[p]

        def one(d, unused):
            back(p, lax.rem(me + d, n)).start()
            return unused

        lax.fori_loop(1, n, one, 0)
        ret[lo:hi, my_slot] = grads[lo:hi, my_rows, :]

    def compute():
        row = lax.broadcasted_iota(jnp.int32, (rows, cells), 0)
        col = lax.broadcasted_iota(jnp.int32, (rows, cells), 1)
        got_slot = jnp.minimum(my_slot, work - 2)
        spare = jnp.where(
            jnp.full((rows_dev, cells), my_slot) < work - 1, keep_got[got_slot], keep_own[0]
        )
        scale = jnp.where(full, keep_own[my_slot], spare)[:1]
        wait_phase(0)
        zeta[...] = jnp.dot(
            kernel[...], fields[0], precision=lax.Precision.HIGHEST,
            preferred_element_type=jnp.float32,
        )
        wait_phase(1)

        def retreat(step, carry, window):
            adj_u, adj_s, adj_f = carry
            total_s = adj_s - STEP * forward_diff(adj_u, row, col)
            total[window * SUB + SUB - 1 - step] = total_s
            adj_f = adj_f + STEP * adj_u
            adj_u = BETA * adj_u + backward_diff(zeta[...] * total_s, row, col)
            return adj_u, GAMMA * total_s, adj_f

        carry = (fields[1], fields[2], jnp.zeros((rows, cells), jnp.float32))
        for window in range(WINDOWS - 1, -1, -1):
            carry = lax.fori_loop(0, SUB, functools.partial(retreat, window=window), carry)
            if window > 0:
                carry = (carry[0], carry[1] * scale, carry[2])
        grads[0] = carry[0]
        grads[1] = carry[1]
        grads[2] = carry[2]
        send_back(0)
        wait_phase(2)

        def advance(step, carry, window):
            u_now, s_now, adj_z = carry
            strain = forward_diff(u_now, row, col)
            s_now = GAMMA * s_now + zeta[...] * strain
            u_now = BETA * u_now - STEP * backward_diff(s_now, row, col) + STEP * fields[5]
            adj_z = adj_z + total[window * SUB + step] * strain
            return u_now, s_now, adj_z

        carry = (fields[3], fields[4], jnp.zeros((rows, cells), jnp.float32))
        for window in range(WINDOWS):
            if window > 0:
                carry = (carry[0], carry[1] * scale, carry[2])
            carry = lax.fori_loop(0, SUB, functools.partial(advance, window=window), carry)
        grads[3] = lax.dot_general(
            kernel[...], carry[2], (((0,), (0,)), ((), ())),
            precision=lax.Precision.HIGHEST, preferred_element_type=jnp.float32,
        )
        send_back(1)

    when_owner(compute)

    def pass_on(p):
        lo, hi = BACK[p]
        return pltpu.make_async_remote_copy(
            src_ref=ret.at[lo:hi, 0 : work - 1], dst_ref=ret.at[lo:hi, work : 2 * work - 1],
            send_sem=fwd_send.at[p], recv_sem=fwd_recv.at[p],
            device_id=(other, me), device_id_type=MESH,
        )

    for p in range(len(BACK)):
        if stride > 1:
            pl.when(jnp.logical_not(is_owner))(lambda p=p: back_arrive(p, my_slot).wait_recv())

        def taken(d, unused, p=p):
            back_arrive(p, lax.rem(my_slot + d, work)).wait_recv()
            return unused

        lax.fori_loop(1, work, taken, 0)
        pass_on(p).start()

    for p in range(len(PHASES) + 1):
        exchange(p).wait_send()
    for p in range(len(PHASES)):

        def gone(d, unused, p=p):
            slot = lax.rem(my_slot + d, work)
            go(p, slot, slot * stride).wait_send()
            return unused

        lax.fori_loop(1, work, gone, 0)
        if stride > 1:
            pl.when(jnp.logical_not(is_owner))(
                lambda p=p: go(p, my_slot, my_slot * stride).wait_send()
            )

    def returned():
        for p in range(len(BACK)):

            def one(d, unused, p=p):
                back(p, lax.rem(me + d, n)).wait_send()
                return unused

            lax.fori_loop(1, n, one, 0)

    when_owner(returned)
    for p in range(len(BACK)):
        pass_on(p).wait()
    ret[:, 2 * work - 1] = jnp.zeros((GRADS, rows_dev, cells), jnp.float32)


def place_kernel(covered, home, ret, switch, grad_u, grad_s, grad_q, grad_f):
    blocks, rows_dev, cells = switch.shape

    def one(b, unused):
        slot = home[b]
        live = jnp.full((rows_dev, cells), covered[b]) == 1
        coef = jnp.where(switch[b] == 1, PLASTIC, VISCOUS)
        grad_u[b] = jnp.where(live, ret[0, slot], 0.0)
        grad_s[b] = jnp.where(live, ret[1, slot], 0.0)
        grad_f[b] = jnp.where(live, ret[2, slot], 0.0)
        grad_q[b] = jnp.where(live, ret[3, slot] * coef, 0.0)
        return unused

    lax.fori_loop(0, blocks, one, 0, unroll=8)


def shards(
    velocity, stress, thickness, forcing, switch, covered, reinit, cot_velocity, cot_stress, kernel
):
    blocks, rows_dev, cells = velocity.shape
    n = lax.axis_size("ice")
    work = COVERED // lax.axis_size("ocean")
    rows = kernel.shape[0]
    smem = pl.BlockSpec(memory_space=pltpu.SMEM)
    vmem = pl.BlockSpec(memory_space=pltpu.VMEM)
    i32, f32 = jnp.int32, jnp.float32
    tile = (rows_dev, cells)

    idx, keep, home, heavy = pl.pallas_call(
        functools.partial(plan_kernel, work),
        out_shape=[
            jax.ShapeDtypeStruct((2 * work,), i32),
            jax.ShapeDtypeStruct((2 * work,), i32),
            jax.ShapeDtypeStruct((blocks,), i32),
            jax.ShapeDtypeStruct((1,), i32),
        ],
        in_specs=[smem] * 2,
        out_specs=[smem] * 4,
    )(covered, reinit)

    ret = pl.pallas_call(
        functools.partial(work_kernel, n, work),
        out_shape=jax.ShapeDtypeStruct((GRADS, 2 * work) + tile, f32),
        in_specs=[smem] * 3 + [vmem] * 8,
        out_specs=vmem,
        scratch_shapes=[
            pltpu.VMEM((FIELDS, work) + tile, f32),
            pltpu.VMEM((FIELDS, work - 1) + tile, f32),
            pltpu.VMEM((FIELDS, work - 1) + tile, f32),
            pltpu.VMEM((work,) + tile, f32),
            pltpu.VMEM((work - 1,) + tile, f32),
            pltpu.VMEM((work - 1,) + tile, f32),
            pltpu.VMEM((work, FIELDS) + tile, f32),
            pltpu.VMEM((FIELDS, rows, cells), f32),
            pltpu.VMEM((rows, cells), f32),
            pltpu.VMEM((WINDOWS * SUB, rows, cells), f32),
            pltpu.VMEM((GRADS, rows, cells), f32),
            pltpu.SemaphoreType.DMA((len(PHASES) + 1,)),
            pltpu.SemaphoreType.DMA((len(PHASES) + 1,)),
            pltpu.SemaphoreType.DMA((len(PHASES), work)),
            pltpu.SemaphoreType.DMA((len(PHASES), n)),
            pltpu.SemaphoreType.DMA((len(BACK), n)),
            pltpu.SemaphoreType.DMA((len(BACK), work)),
            pltpu.SemaphoreType.DMA((len(BACK),)),
            pltpu.SemaphoreType.DMA((len(BACK),)),
        ],
        compiler_params=pltpu.CompilerParams(
            collective_id=0, has_side_effects=True, vmem_limit_bytes=40 << 20
        ),
    )(idx, keep, heavy, velocity, stress, thickness, forcing, switch, cot_velocity, cot_stress, kernel)

    field = jax.ShapeDtypeStruct(velocity.shape, f32)
    grad_u, grad_s, grad_q, grad_f = pl.pallas_call(
        place_kernel,
        out_shape=[field] * 4,
        in_specs=[smem] * 2 + [vmem] * 2,
        out_specs=[vmem] * 4,
    )(covered, home, ret, switch)
    return grad_u, grad_s, grad_q, grad_f


def solution(mesh):
    split = P("ocean", "ice", None)
    return jax.shard_map(
        shards,
        mesh=mesh,
        in_specs=(split,) * 5 + (P("ocean"),) * 2 + (split,) * 2 + (P(),),
        out_specs=(split,) * 4,
        check_vma=False,
    )
```

```python
import functools

import jax
import jax.numpy as jnp
from jax import lax
from jax.experimental import pallas as pl
from jax.experimental.pallas import tpu as pltpu
from jax.sharding import PartitionSpec as P

SUB = 8
WINDOWS = 2
COVERED = 32

PLASTIC = 0.25
VISCOUS = 1.0
GAMMA = 0.6
BETA = 0.9
STEP = 0.04

MESH = pl.DeviceIdType.MESH
FIELDS = 6
PHASES = ((0, 1), (1, 3), (3, 6))
GRADS = 4
BACK = ((0, 3), (3, 4))


def forward_diff(x, row, col):
    upper = jnp.where(row == 0, 0.0, pltpu.roll(x, 1, 0))
    left = jnp.where(col == 0, 0.0, pltpu.roll(x, 1, 1))
    return 2.0 * x - upper - left


def backward_diff(x, row, col):
    rows, cells = x.shape
    lower = jnp.where(row == rows - 1, 0.0, pltpu.roll(x, rows - 1, 0))
    right = jnp.where(col == cells - 1, 0.0, pltpu.roll(x, cells - 1, 1))
    return 2.0 * x - lower - right


def work_kernel(
    n, work, covered_in, reinit_in, *refs
):
    operands, ret, inputs, (covered, reinit, idx_row, idx), rest = (
        refs[:8], refs[8], refs[9:17], refs[17:21], refs[21:]
    )
    velo, stress, thick, force, switch, cot_u, cot_s, kernel = inputs
    (
        own, over, got, keep_own, keep_over, keep_got, send, fields, zeta, total, grads,
        in_sem, plan_sem, ex_send, ex_recv, go_send, go_recv, back_send, back_recv, own_sem,
        fwd_send, fwd_recv,
    ) = rest
    ocean = lax.axis_index("ocean")
    me = lax.axis_index("ice")
    other = 1 - ocean
    stride = n // work
    rows_dev = velo.shape[1]
    cells = velo.shape[2]
    rows = kernel.shape[0]
    my_slot = me // stride
    is_owner = me % stride == 0

    def when_owner(body):
        if stride == 1:
            body()
        else:
            pl.when(is_owner)(body)

    plan_in = (
        pltpu.make_async_copy(covered_in, covered, plan_sem.at[0]),
        pltpu.make_async_copy(reinit_in, reinit, plan_sem.at[1]),
    )
    fetch = [
        pltpu.make_async_copy(operands[i], inputs[i], in_sem.at[i]) for i in range(len(operands))
    ]
    for copy in plan_in:
        copy.start()
    for i in (2, 4, 5, 6, 0, 1, 3, 7):
        fetch[i].start()

    barrier = pltpu.get_barrier_semaphore()

    def greet(d, unused):
        pl.semaphore_signal(
            barrier, inc=1, device_id=(ocean, lax.rem(me + d, n)), device_id_type=MESH
        )
        return unused

    pl.semaphore_signal(barrier, inc=1, device_id=(other, me), device_id_type=MESH)
    lax.fori_loop(1, n, greet, 0)

    for copy in plan_in:
        copy.wait()
    blocks = covered.shape[1]
    ones = jnp.broadcast_to(covered[...].astype(jnp.float32), (8, blocks))
    upto = (
        lax.broadcasted_iota(jnp.int32, (blocks, blocks), 1)
        <= lax.broadcasted_iota(jnp.int32, (blocks, blocks), 0)
    ).astype(jnp.float32)
    tally = lax.dot_general(
        upto, ones, (((1,), (1,)), ((), ())), preferred_element_type=jnp.float32
    )
    ranks = lax.broadcasted_iota(jnp.int32, (blocks, cells), 1).astype(jnp.float32)
    before = jnp.where(jnp.broadcast_to(tally[:, :1], (blocks, cells)) <= ranks, 1, 0)
    idx_row[...] = jnp.minimum(jnp.sum(before, axis=0, keepdims=True), blocks - 1)
    to_scalars = pltpu.make_async_copy(idx_row, idx, plan_sem.at[2])
    to_scalars.start()
    count = jnp.sum(ones, axis=1, keepdims=True)[:1]
    full = jnp.broadcast_to(count, (rows_dev, cells)) > work + 0.0

    fetched = ((2, 4), (5, 6), (0, 1, 3))
    sources = (None, cot_u, cot_s, velo, stress, force)

    def pack(dst, k, rank, p):
        b = idx[0, rank]
        for f in range(*PHASES[p]):
            if f == 0:
                dst[f, k] = thick[b] * jnp.where(switch[b] == 1, PLASTIC, VISCOUS)
            else:
                dst[f, k] = sources[f][b]

    def pack_keep(dst, k, rank):
        kept = (1 - reinit[0, idx[0, rank]]).astype(jnp.float32)
        dst[k] = jnp.full((rows_dev, cells), kept)

    def exchange(p):
        if p == len(PHASES):
            src, dst = keep_over, keep_got
        else:
            lo, hi = PHASES[p]
            src, dst = over.at[lo:hi], got.at[lo:hi]
        return pltpu.make_async_remote_copy(
            src_ref=src, dst_ref=dst, send_sem=ex_send.at[p], recv_sem=ex_recv.at[p],
            device_id=(other, me), device_id_type=MESH,
        )

    to_scalars.wait()
    for p in range(len(PHASES)):
        for i in fetched[p]:
            fetch[i].wait()
        for k in range(work - 1):
            pack(over, k, work + k, p)
        if p == 0:
            pl.semaphore_wait(barrier, n)
        exchange(p).start()
    for k in range(work - 1):
        pack_keep(keep_over, k, work + k)
    exchange(len(PHASES)).start()
    for p in range(len(PHASES)):
        for k in range(work):
            pack(own, k, k, p)
    for k in range(work):
        pack_keep(keep_own, k, k)

    my_rows = pl.ds(pl.multiple_of(me * rows_dev, rows_dev), rows_dev)

    def go(p, slot, target):
        lo, hi = PHASES[p]
        return pltpu.make_async_remote_copy(
            src_ref=send.at[slot, lo:hi], dst_ref=fields.at[lo:hi, my_rows, :],
            send_sem=go_send.at[p, slot], recv_sem=go_recv.at[p, me],
            device_id=(ocean, target), device_id_type=MESH,
        )

    def arrive(p, j):
        lo, hi = PHASES[p]
        there = pl.ds(pl.multiple_of(j * rows_dev, rows_dev), rows_dev)
        return pltpu.make_async_remote_copy(
            src_ref=send.at[0, lo:hi], dst_ref=fields.at[lo:hi, there, :],
            send_sem=go_send.at[p, 0], recv_sem=go_recv.at[p, j],
            device_id=(ocean, j), device_id_type=MESH,
        )

    for p, (lo, hi) in enumerate(PHASES):
        exchange(p).wait_recv()
        for k in range(work):
            for f in range(lo, hi):
                rest = got[f, k] if k < work - 1 else own[f, 0]
                send[k, f] = jnp.where(full, own[f, k], rest)

        def start(d, unused, p=p):
            slot = lax.rem(my_slot + d, work)
            go(p, slot, slot * stride).start()
            return unused

        lax.fori_loop(1, work, start, 0)

        def local(lo=lo, hi=hi):
            fields[lo:hi, my_rows, :] = send[my_slot, lo:hi]

        when_owner(local)
        if stride > 1:
            pl.when(jnp.logical_not(is_owner))(lambda p=p: go(p, my_slot, my_slot * stride).start())
    exchange(len(PHASES)).wait_recv()

    def wait_phase(p):
        def one(d, unused):
            arrive(p, lax.rem(me + n - d, n)).wait_recv()
            return unused

        lax.fori_loop(1, n, one, 0)

    def back(p, j):
        lo, hi = BACK[p]
        there = pl.ds(pl.multiple_of(j * rows_dev, rows_dev), rows_dev)
        return pltpu.make_async_remote_copy(
            src_ref=grads.at[lo:hi, there, :], dst_ref=ret.at[lo:hi, my_slot],
            send_sem=back_send.at[p, j], recv_sem=back_recv.at[p, my_slot],
            device_id=(ocean, j), device_id_type=MESH,
        )

    def back_own(p):
        lo, hi = BACK[p]
        return pltpu.make_async_copy(
            grads.at[lo:hi, my_rows, :], ret.at[lo:hi, my_slot], own_sem.at[p]
        )

    def back_arrive(p, slot):
        lo, hi = BACK[p]
        return pltpu.make_async_remote_copy(
            src_ref=grads.at[lo:hi, my_rows, :], dst_ref=ret.at[lo:hi, slot],
            send_sem=back_send.at[p, 0], recv_sem=back_recv.at[p, slot],
            device_id=(ocean, slot * stride), device_id_type=MESH,
        )

    def send_back(p):
        lo, hi = BACK[p]

        def one(d, unused):
            back(p, lax.rem(me + d, n)).start()
            return unused

        lax.fori_loop(1, n, one, 0)
        back_own(p).start()

    def compute():
        row = lax.broadcasted_iota(jnp.int32, (rows, cells), 0)
        col = lax.broadcasted_iota(jnp.int32, (rows, cells), 1)
        got_slot = jnp.minimum(my_slot, work - 2)
        spare = jnp.where(
            jnp.full((rows_dev, cells), my_slot) < work - 1, keep_got[got_slot], keep_own[0]
        )
        scale = jnp.where(full, keep_own[my_slot], spare)[:1]
        fetch[7].wait()
        wait_phase(0)
        zeta[...] = jnp.dot(
            kernel[...], fields[0], precision=lax.Precision.HIGHEST,
            preferred_element_type=jnp.float32,
        )
        wait_phase(1)

        def retreat(step, carry, window):
            adj_u, adj_s, adj_f = carry
            total_s = adj_s - STEP * forward_diff(adj_u, row, col)
            total[window * SUB + SUB - 1 - step] = total_s
            adj_f = adj_f + STEP * adj_u
            adj_u = BETA * adj_u + backward_diff(zeta[...] * total_s, row, col)
            return adj_u, GAMMA * total_s, adj_f

        carry = (fields[1], fields[2], jnp.zeros((rows, cells), jnp.float32))
        for window in range(WINDOWS - 1, -1, -1):
            carry = lax.fori_loop(0, SUB, functools.partial(retreat, window=window), carry)
            if window > 0:
                carry = (carry[0], carry[1] * scale, carry[2])
        grads[0] = carry[0]
        grads[1] = carry[1]
        grads[2] = carry[2]
        send_back(0)
        wait_phase(2)

        def advance(step, carry, window):
            u_now, s_now, adj_z = carry
            strain = forward_diff(u_now, row, col)
            s_now = GAMMA * s_now + zeta[...] * strain
            u_now = BETA * u_now - STEP * backward_diff(s_now, row, col) + STEP * fields[5]
            adj_z = adj_z + total[window * SUB + step] * strain
            return u_now, s_now, adj_z

        carry = (fields[3], fields[4], jnp.zeros((rows, cells), jnp.float32))
        for window in range(WINDOWS):
            if window > 0:
                carry = (carry[0], carry[1] * scale, carry[2])
            carry = lax.fori_loop(0, SUB, functools.partial(advance, window=window), carry)
        grads[3] = lax.dot_general(
            kernel[...], carry[2], (((0,), (0,)), ((), ())),
            precision=lax.Precision.HIGHEST, preferred_element_type=jnp.float32,
        )
        send_back(1)

    when_owner(compute)
    if stride > 1:
        pl.when(jnp.logical_not(is_owner))(lambda: fetch[7].wait())

    def pass_on(p):
        lo, hi = BACK[p]
        return pltpu.make_async_remote_copy(
            src_ref=ret.at[lo:hi, 0 : work - 1], dst_ref=ret.at[lo:hi, work : 2 * work - 1],
            send_sem=fwd_send.at[p], recv_sem=fwd_recv.at[p],
            device_id=(other, me), device_id_type=MESH,
        )

    for p in range(len(BACK)):
        if stride > 1:
            pl.when(jnp.logical_not(is_owner))(lambda p=p: back_arrive(p, my_slot).wait_recv())

        def taken(d, unused, p=p):
            back_arrive(p, lax.rem(my_slot + d, work)).wait_recv()
            return unused

        lax.fori_loop(1, work, taken, 0)
        when_owner(lambda p=p: back_own(p).wait())
        pass_on(p).start()

    for p in range(len(PHASES) + 1):
        exchange(p).wait_send()
    for p in range(len(PHASES)):

        def gone(d, unused, p=p):
            slot = lax.rem(my_slot + d, work)
            go(p, slot, slot * stride).wait_send()
            return unused

        lax.fori_loop(1, work, gone, 0)
        if stride > 1:
            pl.when(jnp.logical_not(is_owner))(
                lambda p=p: go(p, my_slot, my_slot * stride).wait_send()
            )

    def returned():
        for p in range(len(BACK)):

            def one(d, unused, p=p):
                back(p, lax.rem(me + d, n)).wait_send()
                return unused

            lax.fori_loop(1, n, one, 0)

    when_owner(returned)
    for p in range(len(BACK)):
        pass_on(p).wait()


def place_kernel(work, covered_in, ret_in, switch_in, *refs):
    outs, covered, ret, switch, placed, in_sem, out_sem = refs[:4], *refs[4:]
    blocks, rows_dev, cells = switch.shape
    fetch = [
        pltpu.make_async_copy(covered_in, covered, in_sem.at[0]),
        pltpu.make_async_copy(switch_in, switch, in_sem.at[1]),
    ] + [
        pltpu.make_async_copy(ret_in.at[f], ret.at[f], in_sem.at[2 + f]) for f in range(GRADS)
    ]
    for copy in fetch:
        copy.start()
    fetch[0].wait()
    rank = jnp.int32(0)
    ranks = []
    for b in range(blocks):
        ranks.append(rank)
        rank = rank + covered[0, b]
    many = rank > work
    homes = [
        jnp.where(many, jnp.minimum(r, 2 * work - 2), work - 1) for r in ranks
    ]
    fetch[1].wait()
    for f in range(GRADS):
        fetch[2 + f].wait()
        for b in range(blocks):
            live = jnp.full((rows_dev, cells), covered[0, b]) == 1
            value = ret[f, homes[b]]
            if f == GRADS - 1:
                value = value * jnp.where(switch[b] == 1, PLASTIC, VISCOUS)
            placed[f, b] = jnp.where(live, value, 0.0)
        pltpu.make_async_copy(placed.at[f], outs[f], out_sem.at[f]).start()
    for f in range(GRADS):
        pltpu.make_async_copy(placed.at[f], outs[f], out_sem.at[f]).wait()


def shards(
    velocity, stress, thickness, forcing, switch, covered, reinit, cot_velocity, cot_stress, kernel
):
    blocks, rows_dev, cells = velocity.shape
    n = lax.axis_size("ice")
    work = COVERED // lax.axis_size("ocean")
    rows = kernel.shape[0]
    hbm = pl.BlockSpec(memory_space=pl.ANY)
    i32, f32 = jnp.int32, jnp.float32
    tile = (rows_dev, cells)
    covered = covered.reshape(1, blocks)
    reinit = reinit.reshape(1, blocks)
    operands = (
        velocity, stress, thickness, forcing, switch, cot_velocity, cot_stress, kernel
    )

    ret = pl.pallas_call(
        functools.partial(work_kernel, n, work),
        out_shape=jax.ShapeDtypeStruct((GRADS, 2 * work - 1) + tile, f32),
        in_specs=[hbm] * 10,
        out_specs=hbm,
        scratch_shapes=[pltpu.VMEM(x.shape, x.dtype) for x in operands]
        + [
            pltpu.VMEM((1, blocks), i32),
            pltpu.SMEM((1, blocks), i32),
            pltpu.VMEM((1, cells), i32),
            pltpu.SMEM((1, cells), i32),
            pltpu.VMEM((FIELDS, work) + tile, f32),
            pltpu.VMEM((FIELDS, work - 1) + tile, f32),
            pltpu.VMEM((FIELDS, work - 1) + tile, f32),
            pltpu.VMEM((work,) + tile, f32),
            pltpu.VMEM((work - 1,) + tile, f32),
            pltpu.VMEM((work - 1,) + tile, f32),
            pltpu.VMEM((work, FIELDS) + tile, f32),
            pltpu.VMEM((FIELDS, rows, cells), f32),
            pltpu.VMEM((rows, cells), f32),
            pltpu.VMEM((WINDOWS * SUB, rows, cells), f32),
            pltpu.VMEM((GRADS, rows, cells), f32),
            pltpu.SemaphoreType.DMA((len(operands),)),
            pltpu.SemaphoreType.DMA((3,)),
            pltpu.SemaphoreType.DMA((len(PHASES) + 1,)),
            pltpu.SemaphoreType.DMA((len(PHASES) + 1,)),
            pltpu.SemaphoreType.DMA((len(PHASES), work)),
            pltpu.SemaphoreType.DMA((len(PHASES), n)),
            pltpu.SemaphoreType.DMA((len(BACK), n)),
            pltpu.SemaphoreType.DMA((len(BACK), work)),
            pltpu.SemaphoreType.DMA((len(BACK),)),
            pltpu.SemaphoreType.DMA((len(BACK),)),
            pltpu.SemaphoreType.DMA((len(BACK),)),
        ],
        compiler_params=pltpu.CompilerParams(
            collective_id=0, has_side_effects=True, vmem_limit_bytes=64 << 20
        ),
    )(covered, reinit, *operands)

    field = jax.ShapeDtypeStruct(velocity.shape, f32)
    grad_u, grad_s, grad_f, grad_q = pl.pallas_call(
        functools.partial(place_kernel, work),
        out_shape=[field] * GRADS,
        in_specs=[hbm] * 3,
        out_specs=[hbm] * GRADS,
        scratch_shapes=[
            pltpu.SMEM((1, blocks), i32),
            pltpu.VMEM(ret.shape, f32),
            pltpu.VMEM(switch.shape, i32),
            pltpu.VMEM((GRADS,) + velocity.shape, f32),
            pltpu.SemaphoreType.DMA((2 + GRADS,)),
            pltpu.SemaphoreType.DMA((GRADS,)),
        ],
        compiler_params=pltpu.CompilerParams(vmem_limit_bytes=64 << 20),
    )(covered, ret, switch)
    return grad_u, grad_s, grad_q, grad_f


def solution(mesh):
    split = P("ocean", "ice", None)
    return jax.shard_map(
        shards,
        mesh=mesh,
        in_specs=(split,) * 5 + (P("ocean"),) * 2 + (split,) * 2 + (P(),),
        out_specs=(split,) * 4,
        check_vma=False,
    )
```

```python
import functools

import jax
import jax.numpy as jnp
from jax import lax
from jax.experimental import pallas as pl
from jax.experimental.pallas import tpu as pltpu
from jax.sharding import PartitionSpec as P

SUB = 8
WINDOWS = 2
COVERED = 32

PLASTIC = 0.25
VISCOUS = 1.0
GAMMA = 0.6
BETA = 0.9
STEP = 0.04

MESH = pl.DeviceIdType.MESH
FIELDS = 6
PHASES = ((0, 1), (1, 3), (3, 6))
GRADS = 4
BACK = ((0, 3), (3, 4))


def forward_diff(x, row, col):
    upper = jnp.where(row == 0, 0.0, pltpu.roll(x, 1, 0))
    left = jnp.where(col == 0, 0.0, pltpu.roll(x, 1, 1))
    return 2.0 * x - upper - left


def backward_diff(x, row, col):
    rows, cells = x.shape
    lower = jnp.where(row == rows - 1, 0.0, pltpu.roll(x, rows - 1, 0))
    right = jnp.where(col == cells - 1, 0.0, pltpu.roll(x, cells - 1, 1))
    return 2.0 * x - lower - right


def work_kernel(
    n, work, covered_in, reinit_in, *refs
):
    operands, ret, inputs, (covered, reinit, idx_row, idx), rest = (
        refs[:8], refs[8], refs[9:17], refs[17:21], refs[21:]
    )
    velo, stress, thick, force, switch, cot_u, cot_s, kernel = inputs
    (
        own, over, got, keep_own, keep_over, keep_got, send, fields, zeta, total, grads,
        in_sem, plan_sem, ex_send, ex_recv, go_send, go_recv, back_send, back_recv, own_sem,
        fwd_send, fwd_recv,
    ) = rest
    ocean = lax.axis_index("ocean")
    me = lax.axis_index("ice")
    other = 1 - ocean
    stride = n // work
    rows_dev = velo.shape[1]
    cells = velo.shape[2]
    rows = kernel.shape[0]
    my_slot = me // stride
    is_owner = me % stride == 0

    def when_owner(body):
        if stride == 1:
            body()
        else:
            pl.when(is_owner)(body)

    plan_in = (
        pltpu.make_async_copy(covered_in, covered, plan_sem.at[0]),
        pltpu.make_async_copy(reinit_in, reinit, plan_sem.at[1]),
    )
    fetch = [
        pltpu.make_async_copy(operands[i], inputs[i], in_sem.at[i]) for i in range(len(operands))
    ]
    for copy in plan_in:
        copy.start()
    for i in (2, 4, 5, 6, 0, 1, 3, 7):
        fetch[i].start()

    barrier = pltpu.get_barrier_semaphore()

    def greet(d, unused):
        pl.semaphore_signal(
            barrier, inc=1, device_id=(ocean, lax.rem(me + d, n)), device_id_type=MESH
        )
        return unused

    pl.semaphore_signal(barrier, inc=1, device_id=(other, me), device_id_type=MESH)
    lax.fori_loop(1, n, greet, 0)

    for copy in plan_in:
        copy.wait()
    blocks = covered.shape[1]
    ones = jnp.broadcast_to(covered[...].astype(jnp.float32), (8, blocks))
    upto = (
        lax.broadcasted_iota(jnp.int32, (blocks, blocks), 1)
        <= lax.broadcasted_iota(jnp.int32, (blocks, blocks), 0)
    ).astype(jnp.float32)
    tally = lax.dot_general(
        upto, ones, (((1,), (1,)), ((), ())), preferred_element_type=jnp.float32
    )
    ranks = lax.broadcasted_iota(jnp.int32, (blocks, cells), 1).astype(jnp.float32)
    before = jnp.where(jnp.broadcast_to(tally[:, :1], (blocks, cells)) <= ranks, 1, 0)
    idx_row[...] = jnp.minimum(jnp.sum(before, axis=0, keepdims=True), blocks - 1)
    to_scalars = pltpu.make_async_copy(idx_row, idx, plan_sem.at[2])
    to_scalars.start()
    count = jnp.sum(ones, axis=1, keepdims=True)[:1]
    full = jnp.broadcast_to(count, (rows_dev, cells)) > work + 0.0

    fetched = ((2, 4), (5, 6), (0, 1, 3))
    sources = (None, cot_u, cot_s, velo, stress, force)

    def pack(dst, k, rank, p):
        b = idx[0, rank]
        for f in range(*PHASES[p]):
            if f == 0:
                dst[f, k] = thick[b] * jnp.where(switch[b] == 1, PLASTIC, VISCOUS)
            else:
                dst[f, k] = sources[f][b]

    def pack_keep(dst, k, rank):
        kept = (1 - reinit[0, idx[0, rank]]).astype(jnp.float32)
        dst[k] = jnp.full((rows_dev, cells), kept)

    def exchange(p):
        if p == len(PHASES):
            src, dst = keep_over, keep_got
        else:
            lo, hi = PHASES[p]
            src, dst = over.at[lo:hi], got.at[lo:hi]
        return pltpu.make_async_remote_copy(
            src_ref=src, dst_ref=dst, send_sem=ex_send.at[p], recv_sem=ex_recv.at[p],
            device_id=(other, me), device_id_type=MESH,
        )

    to_scalars.wait()

    def pack_phase(p):
        for i in fetched[p]:
            fetch[i].wait()
        for k in range(work - 1):
            pack(over, k, work + k, p)
        if p == 0:
            pl.semaphore_wait(barrier, n)
        exchange(p).start()
        for k in range(work):
            pack(own, k, k, p)

    def pack_keeps():
        for k in range(work - 1):
            pack_keep(keep_over, k, work + k)
        exchange(len(PHASES)).start()
        for k in range(work):
            pack_keep(keep_own, k, k)

    my_rows = pl.ds(pl.multiple_of(me * rows_dev, rows_dev), rows_dev)

    def go(p, slot, target):
        lo, hi = PHASES[p]
        return pltpu.make_async_remote_copy(
            src_ref=send.at[slot, lo:hi], dst_ref=fields.at[lo:hi, my_rows, :],
            send_sem=go_send.at[p, slot], recv_sem=go_recv.at[p, me],
            device_id=(ocean, target), device_id_type=MESH,
        )

    def arrive(p, j):
        lo, hi = PHASES[p]
        there = pl.ds(pl.multiple_of(j * rows_dev, rows_dev), rows_dev)
        return pltpu.make_async_remote_copy(
            src_ref=send.at[0, lo:hi], dst_ref=fields.at[lo:hi, there, :],
            send_sem=go_send.at[p, 0], recv_sem=go_recv.at[p, j],
            device_id=(ocean, j), device_id_type=MESH,
        )

    pack_phase(0)
    pack_phase(1)
    for p, (lo, hi) in enumerate(PHASES):
        exchange(p).wait_recv()
        for k in range(work):
            for f in range(lo, hi):
                rest = got[f, k] if k < work - 1 else own[f, 0]
                send[k, f] = jnp.where(full, own[f, k], rest)

        def start(d, unused, p=p):
            slot = lax.rem(my_slot + d, work)
            go(p, slot, slot * stride).start()
            return unused

        lax.fori_loop(1, work, start, 0)

        def local(lo=lo, hi=hi):
            fields[lo:hi, my_rows, :] = send[my_slot, lo:hi]

        when_owner(local)
        if stride > 1:
            pl.when(jnp.logical_not(is_owner))(lambda p=p: go(p, my_slot, my_slot * stride).start())
        if p == 0:
            pack_phase(2)
        elif p == 1:
            pack_keeps()
    exchange(len(PHASES)).wait_recv()

    def wait_phase(p):
        def one(d, unused):
            arrive(p, lax.rem(me + n - d, n)).wait_recv()
            return unused

        lax.fori_loop(1, n, one, 0)

    def back(p, j):
        lo, hi = BACK[p]
        there = pl.ds(pl.multiple_of(j * rows_dev, rows_dev), rows_dev)
        return pltpu.make_async_remote_copy(
            src_ref=grads.at[lo:hi, there, :], dst_ref=ret.at[lo:hi, my_slot],
            send_sem=back_send.at[p, j], recv_sem=back_recv.at[p, my_slot],
            device_id=(ocean, j), device_id_type=MESH,
        )

    def back_own(p):
        lo, hi = BACK[p]
        return pltpu.make_async_copy(
            grads.at[lo:hi, my_rows, :], ret.at[lo:hi, my_slot], own_sem.at[p]
        )

    def back_arrive(p, slot):
        lo, hi = BACK[p]
        return pltpu.make_async_remote_copy(
            src_ref=grads.at[lo:hi, my_rows, :], dst_ref=ret.at[lo:hi, slot],
            send_sem=back_send.at[p, 0], recv_sem=back_recv.at[p, slot],
            device_id=(ocean, slot * stride), device_id_type=MESH,
        )

    def send_back(p):
        lo, hi = BACK[p]

        def one(d, unused):
            back(p, lax.rem(me + d, n)).start()
            return unused

        lax.fori_loop(1, n, one, 0)
        back_own(p).start()

    def compute():
        row = lax.broadcasted_iota(jnp.int32, (rows, cells), 0)
        col = lax.broadcasted_iota(jnp.int32, (rows, cells), 1)
        got_slot = jnp.minimum(my_slot, work - 2)
        spare = jnp.where(
            jnp.full((rows_dev, cells), my_slot) < work - 1, keep_got[got_slot], keep_own[0]
        )
        scale = jnp.where(full, keep_own[my_slot], spare)[:1]
        fetch[7].wait()
        wait_phase(0)
        zeta[...] = -STEP * jnp.dot(
            kernel[...], fields[0], precision=lax.Precision.HIGHEST,
            preferred_element_type=jnp.float32,
        )
        wait_phase(1)

        def retreat(carry, step):
            adj, adj_s, adj_f = carry
            total_s = adj_s + forward_diff(adj, row, col)
            total[step] = total_s
            adj_f = adj_f + adj
            adj = BETA * adj + backward_diff(zeta[...] * total_s, row, col)
            return adj, GAMMA * total_s, adj_f

        carry = (-STEP * fields[1], fields[2], jnp.zeros((rows, cells), jnp.float32))
        for step in range(WINDOWS * SUB - 1, -1, -1):
            carry = retreat(carry, step)
            if step > 0 and step % SUB == 0:
                carry = (carry[0], carry[1] * scale, carry[2])
        grads[0] = carry[0] * (-1.0 / STEP)
        grads[1] = carry[1]
        grads[2] = -carry[2]
        send_back(0)
        wait_phase(2)

        def advance(carry, step):
            u_now, r_now, adj_z = carry
            strain = forward_diff(u_now, row, col)
            r_now = GAMMA * r_now + zeta[...] * strain
            u_now = BETA * u_now + backward_diff(r_now, row, col) + fields[5]
            adj_z = adj_z + total[step] * strain
            return u_now, r_now, adj_z

        fields[5] = STEP * fields[5]
        carry = (fields[3], -STEP * fields[4], jnp.zeros((rows, cells), jnp.float32))
        for step in range(WINDOWS * SUB):
            if step > 0 and step % SUB == 0:
                carry = (carry[0], carry[1] * scale, carry[2])
            carry = advance(carry, step)
        grads[3] = lax.dot_general(
            kernel[...], carry[2], (((0,), (0,)), ((), ())),
            precision=lax.Precision.HIGHEST, preferred_element_type=jnp.float32,
        )
        send_back(1)

    when_owner(compute)
    if stride > 1:
        pl.when(jnp.logical_not(is_owner))(lambda: fetch[7].wait())

    def pass_on(p):
        lo, hi = BACK[p]
        return pltpu.make_async_remote_copy(
            src_ref=ret.at[lo:hi, 0 : work - 1], dst_ref=ret.at[lo:hi, work : 2 * work - 1],
            send_sem=fwd_send.at[p], recv_sem=fwd_recv.at[p],
            device_id=(other, me), device_id_type=MESH,
        )

    for p in range(len(BACK)):
        if stride > 1:
            pl.when(jnp.logical_not(is_owner))(lambda p=p: back_arrive(p, my_slot).wait_recv())

        def taken(d, unused, p=p):
            back_arrive(p, lax.rem(my_slot + d, work)).wait_recv()
            return unused

        lax.fori_loop(1, work, taken, 0)
        when_owner(lambda p=p: back_own(p).wait())
        pass_on(p).start()

    for p in range(len(PHASES) + 1):
        exchange(p).wait_send()
    for p in range(len(PHASES)):

        def gone(d, unused, p=p):
            slot = lax.rem(my_slot + d, work)
            go(p, slot, slot * stride).wait_send()
            return unused

        lax.fori_loop(1, work, gone, 0)
        if stride > 1:
            pl.when(jnp.logical_not(is_owner))(
                lambda p=p: go(p, my_slot, my_slot * stride).wait_send()
            )

    def returned():
        for p in range(len(BACK)):

            def one(d, unused, p=p):
                back(p, lax.rem(me + d, n)).wait_send()
                return unused

            lax.fori_loop(1, n, one, 0)

    when_owner(returned)
    for p in range(len(BACK)):
        pass_on(p).wait()


def place_kernel(work, covered_in, ret_in, switch_in, *refs):
    outs, covered, ret, switch, placed, in_sem, out_sem = refs[:4], *refs[4:]
    blocks, rows_dev, cells = switch.shape
    fetch = [
        pltpu.make_async_copy(covered_in, covered, in_sem.at[0]),
        pltpu.make_async_copy(switch_in, switch, in_sem.at[1]),
    ] + [
        pltpu.make_async_copy(ret_in.at[f], ret.at[f], in_sem.at[2 + f]) for f in range(GRADS)
    ]
    for copy in fetch:
        copy.start()
    fetch[0].wait()
    rank = jnp.int32(0)
    ranks = []
    for b in range(blocks):
        ranks.append(rank)
        rank = rank + covered[0, b]
    many = rank > work
    homes = [
        jnp.where(many, jnp.minimum(r, 2 * work - 2), work - 1) for r in ranks
    ]
    fetch[1].wait()
    for f in range(GRADS):
        fetch[2 + f].wait()
        for b in range(blocks):
            live = jnp.full((rows_dev, cells), covered[0, b]) == 1
            value = ret[f, homes[b]]
            if f == GRADS - 1:
                value = value * jnp.where(switch[b] == 1, PLASTIC, VISCOUS)
            placed[f, b] = jnp.where(live, value, 0.0)
        pltpu.make_async_copy(placed.at[f], outs[f], out_sem.at[f]).start()
    for f in range(GRADS):
        pltpu.make_async_copy(placed.at[f], outs[f], out_sem.at[f]).wait()


def shards(
    velocity, stress, thickness, forcing, switch, covered, reinit, cot_velocity, cot_stress, kernel
):
    blocks, rows_dev, cells = velocity.shape
    n = lax.axis_size("ice")
    work = COVERED // lax.axis_size("ocean")
    rows = kernel.shape[0]
    hbm = pl.BlockSpec(memory_space=pl.ANY)
    i32, f32 = jnp.int32, jnp.float32
    tile = (rows_dev, cells)
    covered = covered.reshape(1, blocks)
    reinit = reinit.reshape(1, blocks)
    operands = (
        velocity, stress, thickness, forcing, switch, cot_velocity, cot_stress, kernel
    )

    ret = pl.pallas_call(
        functools.partial(work_kernel, n, work),
        out_shape=jax.ShapeDtypeStruct((GRADS, 2 * work - 1) + tile, f32),
        in_specs=[hbm] * 10,
        out_specs=hbm,
        scratch_shapes=[pltpu.VMEM(x.shape, x.dtype) for x in operands]
        + [
            pltpu.VMEM((1, blocks), i32),
            pltpu.SMEM((1, blocks), i32),
            pltpu.VMEM((1, cells), i32),
            pltpu.SMEM((1, cells), i32),
            pltpu.VMEM((FIELDS, work) + tile, f32),
            pltpu.VMEM((FIELDS, work - 1) + tile, f32),
            pltpu.VMEM((FIELDS, work - 1) + tile, f32),
            pltpu.VMEM((work,) + tile, f32),
            pltpu.VMEM((work - 1,) + tile, f32),
            pltpu.VMEM((work - 1,) + tile, f32),
            pltpu.VMEM((work, FIELDS) + tile, f32),
            pltpu.VMEM((FIELDS, rows, cells), f32),
            pltpu.VMEM((rows, cells), f32),
            pltpu.VMEM((WINDOWS * SUB, rows, cells), f32),
            pltpu.VMEM((GRADS, rows, cells), f32),
            pltpu.SemaphoreType.DMA((len(operands),)),
            pltpu.SemaphoreType.DMA((3,)),
            pltpu.SemaphoreType.DMA((len(PHASES) + 1,)),
            pltpu.SemaphoreType.DMA((len(PHASES) + 1,)),
            pltpu.SemaphoreType.DMA((len(PHASES), work)),
            pltpu.SemaphoreType.DMA((len(PHASES), n)),
            pltpu.SemaphoreType.DMA((len(BACK), n)),
            pltpu.SemaphoreType.DMA((len(BACK), work)),
            pltpu.SemaphoreType.DMA((len(BACK),)),
            pltpu.SemaphoreType.DMA((len(BACK),)),
            pltpu.SemaphoreType.DMA((len(BACK),)),
        ],
        compiler_params=pltpu.CompilerParams(
            collective_id=0, has_side_effects=True, vmem_limit_bytes=64 << 20
        ),
    )(covered, reinit, *operands)

    field = jax.ShapeDtypeStruct(velocity.shape, f32)
    grad_u, grad_s, grad_f, grad_q = pl.pallas_call(
        functools.partial(place_kernel, work),
        out_shape=[field] * GRADS,
        in_specs=[hbm] * 3,
        out_specs=[hbm] * GRADS,
        scratch_shapes=[
            pltpu.SMEM((1, blocks), i32),
            pltpu.VMEM(ret.shape, f32),
            pltpu.VMEM(switch.shape, i32),
            pltpu.VMEM((GRADS,) + velocity.shape, f32),
            pltpu.SemaphoreType.DMA((2 + GRADS,)),
            pltpu.SemaphoreType.DMA((GRADS,)),
        ],
        compiler_params=pltpu.CompilerParams(vmem_limit_bytes=64 << 20),
    )(covered, ret, switch)
    return grad_u, grad_s, grad_q, grad_f


def solution(mesh):
    split = P("ocean", "ice", None)
    return jax.shard_map(
        shards,
        mesh=mesh,
        in_specs=(split,) * 5 + (P("ocean"),) * 2 + (split,) * 2 + (P(),),
        out_specs=(split,) * 4,
        check_vma=False,
    )
```

```python
import functools

import jax
import jax.numpy as jnp
from jax import lax
from jax.experimental import pallas as pl
from jax.experimental.pallas import tpu as pltpu
from jax.sharding import PartitionSpec as P

SUB = 8
WINDOWS = 2
COVERED = 32

PLASTIC = 0.25
VISCOUS = 1.0
GAMMA = 0.6
BETA = 0.9
STEP = 0.04

MESH = pl.DeviceIdType.MESH
FIELDS = 6
PHASES = ((0, 1), (1, 3), (3, 6))
GRADS = 4
BACK = ((0, 3), (3, 4))


SUBLANES = 8


def load_tiles(ref, index, rows):
    count = rows // SUBLANES
    return [ref[index, pl.ds(v, SUBLANES, stride=count), :] for v in range(count)]


def store_tiles(ref, index, tiles):
    for v, tile in enumerate(tiles):
        ref[index, pl.ds(v, SUBLANES, stride=len(tiles)), :] = tile


def forward_diff(tiles, row, col):
    first = jnp.where(row == 0, 0.0, pltpu.roll(tiles[-1], 1, 0))
    out = []
    for v, x in enumerate(tiles):
        upper = tiles[v - 1] if v > 0 else first
        left = jnp.where(col == 0, 0.0, pltpu.roll(x, 1, 1))
        out.append((x + x - upper) - left)
    return out


def backward_diff(tiles, row, col):
    last = jnp.where(row == SUBLANES - 1, 0.0, pltpu.roll(tiles[0], SUBLANES - 1, 0))
    cells = tiles[0].shape[1]
    out = []
    for v, x in enumerate(tiles):
        lower = tiles[v + 1] if v + 1 < len(tiles) else last
        right = jnp.where(col == cells - 1, 0.0, pltpu.roll(x, cells - 1, 1))
        out.append((x + x - lower) - right)
    return out


def far_first(d, n):
    return n // 2 + (1 - 2 * (d % 2)) * ((d + 1) // 2)


def work_kernel(
    n, work, covered_in, reinit_in, *refs
):
    operands, ret, inputs, (covered, reinit, idx_row, idx), rest = (
        refs[:8], refs[8], refs[9:17], refs[17:21], refs[21:]
    )
    velo, stress, thick, force, switch, cot_u, cot_s, kernel = inputs
    (
        own, over, got, keep_own, keep_over, keep_got, send, fields, zeta, total, grads,
        in_sem, plan_sem, ex_send, ex_recv, go_send, go_recv, back_send, back_recv, own_sem,
        fwd_send, fwd_recv,
    ) = rest
    ocean = lax.axis_index("ocean")
    me = lax.axis_index("ice")
    other = 1 - ocean
    stride = n // work
    rows_dev = velo.shape[1]
    cells = velo.shape[2]
    rows = kernel.shape[0]
    my_slot = me // stride
    is_owner = me % stride == 0

    def when_owner(body):
        if stride == 1:
            body()
        else:
            pl.when(is_owner)(body)

    plan_in = (
        pltpu.make_async_copy(covered_in, covered, plan_sem.at[0]),
        pltpu.make_async_copy(reinit_in, reinit, plan_sem.at[1]),
    )
    fetch = [
        pltpu.make_async_copy(operands[i], inputs[i], in_sem.at[i]) for i in range(len(operands))
    ]
    for copy in plan_in:
        copy.start()
    for i in (2, 4, 5, 6, 0, 1, 3, 7):
        fetch[i].start()

    barrier = pltpu.get_barrier_semaphore()

    def greet(d, unused):
        pl.semaphore_signal(
            barrier, inc=1, device_id=(ocean, lax.rem(me + d, n)), device_id_type=MESH
        )
        return unused

    pl.semaphore_signal(barrier, inc=1, device_id=(other, me), device_id_type=MESH)
    lax.fori_loop(1, n, greet, 0)

    for copy in plan_in:
        copy.wait()
    blocks = covered.shape[1]
    ones = jnp.broadcast_to(covered[...].astype(jnp.float32), (8, blocks))
    upto = (
        lax.broadcasted_iota(jnp.int32, (blocks, blocks), 1)
        <= lax.broadcasted_iota(jnp.int32, (blocks, blocks), 0)
    ).astype(jnp.float32)
    tally = lax.dot_general(
        upto, ones, (((1,), (1,)), ((), ())), preferred_element_type=jnp.float32
    )
    ranks = lax.broadcasted_iota(jnp.int32, (blocks, cells), 1).astype(jnp.float32)
    before = jnp.where(jnp.broadcast_to(tally[:, :1], (blocks, cells)) <= ranks, 1, 0)
    idx_row[...] = jnp.minimum(jnp.sum(before, axis=0, keepdims=True), blocks - 1)
    to_scalars = pltpu.make_async_copy(idx_row, idx, plan_sem.at[2])
    to_scalars.start()
    count = jnp.sum(ones, axis=1, keepdims=True)[:1]
    full = jnp.broadcast_to(count, (rows_dev, cells)) > work + 0.0

    fetched = ((2, 4), (5, 6), (0, 1, 3))
    sources = (None, cot_u, cot_s, velo, stress, force)

    def pack(dst, k, rank, p):
        b = idx[0, rank]
        for f in range(*PHASES[p]):
            if f == 0:
                dst[f, k] = thick[b] * jnp.where(switch[b] == 1, PLASTIC, VISCOUS)
            else:
                dst[f, k] = sources[f][b]

    def pack_keep(dst, k, rank):
        kept = (1 - reinit[0, idx[0, rank]]).astype(jnp.float32)
        dst[k] = jnp.full((rows_dev, cells), kept)

    def exchange(p):
        if p == len(PHASES):
            src, dst = keep_over, keep_got
        else:
            lo, hi = PHASES[p]
            src, dst = over.at[lo:hi], got.at[lo:hi]
        return pltpu.make_async_remote_copy(
            src_ref=src, dst_ref=dst, send_sem=ex_send.at[p], recv_sem=ex_recv.at[p],
            device_id=(other, me), device_id_type=MESH,
        )

    to_scalars.wait()

    def pack_phase(p):
        for i in fetched[p]:
            fetch[i].wait()
        for k in range(work - 1):
            pack(over, k, work + k, p)
        if p == 0:
            pl.semaphore_wait(barrier, n)
        exchange(p).start()
        for k in range(work):
            pack(own, k, k, p)

    def pack_keeps():
        for k in range(work - 1):
            pack_keep(keep_over, k, work + k)
        exchange(len(PHASES)).start()
        for k in range(work):
            pack_keep(keep_own, k, k)

    my_rows = pl.ds(pl.multiple_of(me * rows_dev, rows_dev), rows_dev)

    def go(p, slot, target):
        lo, hi = PHASES[p]
        return pltpu.make_async_remote_copy(
            src_ref=send.at[slot, lo:hi], dst_ref=fields.at[lo:hi, my_rows, :],
            send_sem=go_send.at[p, slot], recv_sem=go_recv.at[p, me],
            device_id=(ocean, target), device_id_type=MESH,
        )

    def arrive(p, j):
        lo, hi = PHASES[p]
        there = pl.ds(pl.multiple_of(j * rows_dev, rows_dev), rows_dev)
        return pltpu.make_async_remote_copy(
            src_ref=send.at[0, lo:hi], dst_ref=fields.at[lo:hi, there, :],
            send_sem=go_send.at[p, 0], recv_sem=go_recv.at[p, j],
            device_id=(ocean, j), device_id_type=MESH,
        )

    pack_phase(0)
    pack_phase(1)
    for p, (lo, hi) in enumerate(PHASES):
        exchange(p).wait_recv()
        for k in range(work):
            for f in range(lo, hi):
                rest = got[f, k] if k < work - 1 else own[f, 0]
                send[k, f] = jnp.where(full, own[f, k], rest)

        def start(d, unused, p=p):
            slot = lax.rem(my_slot + far_first(d, work), work)
            go(p, slot, slot * stride).start()
            return unused

        lax.fori_loop(0, work - 1, start, 0)

        def local(lo=lo, hi=hi):
            fields[lo:hi, my_rows, :] = send[my_slot, lo:hi]

        when_owner(local)
        if stride > 1:
            pl.when(jnp.logical_not(is_owner))(lambda p=p: go(p, my_slot, my_slot * stride).start())
        if p == 0:
            pack_phase(2)
        elif p == 1:
            pack_keeps()
    exchange(len(PHASES)).wait_recv()

    def wait_phase(p):
        def one(d, unused):
            arrive(p, lax.rem(me + n - d, n)).wait_recv()
            return unused

        lax.fori_loop(1, n, one, 0)

    def back(p, j):
        lo, hi = BACK[p]
        there = pl.ds(pl.multiple_of(j * rows_dev, rows_dev), rows_dev)
        return pltpu.make_async_remote_copy(
            src_ref=grads.at[lo:hi, there, :], dst_ref=ret.at[lo:hi, my_slot],
            send_sem=back_send.at[p, j], recv_sem=back_recv.at[p, my_slot],
            device_id=(ocean, j), device_id_type=MESH,
        )

    def back_own(p):
        lo, hi = BACK[p]
        return pltpu.make_async_copy(
            grads.at[lo:hi, my_rows, :], ret.at[lo:hi, my_slot], own_sem.at[p]
        )

    def back_arrive(p, slot):
        lo, hi = BACK[p]
        return pltpu.make_async_remote_copy(
            src_ref=grads.at[lo:hi, my_rows, :], dst_ref=ret.at[lo:hi, slot],
            send_sem=back_send.at[p, 0], recv_sem=back_recv.at[p, slot],
            device_id=(ocean, slot * stride), device_id_type=MESH,
        )

    def send_back(p):
        lo, hi = BACK[p]

        def one(d, unused):
            back(p, lax.rem(me + far_first(d, n), n)).start()
            return unused

        lax.fori_loop(0, n - 1, one, 0)
        back_own(p).start()

    def compute():
        row = lax.broadcasted_iota(jnp.int32, (SUBLANES, cells), 0)
        col = lax.broadcasted_iota(jnp.int32, (SUBLANES, cells), 1)
        got_slot = jnp.minimum(my_slot, work - 2)
        spare = jnp.where(
            jnp.full((rows_dev, cells), my_slot) < work - 1, keep_got[got_slot], keep_own[0]
        )
        scale = jnp.where(full, keep_own[my_slot], spare)[:1]
        scale = jnp.broadcast_to(scale, (SUBLANES, cells))
        fetch[7].wait()
        wait_phase(0)
        zeta[0] = -STEP * jnp.dot(
            kernel[...], fields[0], precision=lax.Precision.HIGHEST,
            preferred_element_type=jnp.float32,
        )
        wait_phase(1)
        tiles = range(rows // SUBLANES)
        blank = jnp.zeros((SUBLANES, cells), jnp.float32)
        scaled = load_tiles(zeta, 0, rows)

        adj = [-STEP * x for x in load_tiles(fields, 1, rows)]
        adj_s = load_tiles(fields, 2, rows)
        adj_f = [blank for v in tiles]
        for step in range(WINDOWS * SUB - 1, -1, -1):
            diff = forward_diff(adj, row, col)
            total_s = [adj_s[v] + diff[v] for v in tiles]
            for v in tiles:
                total[step, v] = total_s[v]
            adj_f = [adj_f[v] + adj[v] for v in tiles]
            diff = backward_diff([scaled[v] * total_s[v] for v in tiles], row, col)
            adj = [BETA * adj[v] + diff[v] for v in tiles]
            adj_s = [GAMMA * total_s[v] for v in tiles]
            if step > 0 and step % SUB == 0:
                adj_s = [x * scale for x in adj_s]
        store_tiles(grads, 0, [x * (-1.0 / STEP) for x in adj])
        store_tiles(grads, 1, adj_s)
        store_tiles(grads, 2, [-x for x in adj_f])
        send_back(0)
        wait_phase(2)

        u_now = load_tiles(fields, 3, rows)
        r_now = [-STEP * x for x in load_tiles(fields, 4, rows)]
        pushed = [STEP * x for x in load_tiles(fields, 5, rows)]
        scaled = load_tiles(zeta, 0, rows)
        adj_z = [blank for v in tiles]
        for step in range(WINDOWS * SUB):
            if step > 0 and step % SUB == 0:
                r_now = [x * scale for x in r_now]
            strain = forward_diff(u_now, row, col)
            adj_z = [adj_z[v] + total[step, v] * strain[v] for v in tiles]
            r_now = [GAMMA * r_now[v] + scaled[v] * strain[v] for v in tiles]
            if step < WINDOWS * SUB - 1:
                diff = backward_diff(r_now, row, col)
                u_now = [BETA * u_now[v] + diff[v] + pushed[v] for v in tiles]
        store_tiles(zeta, 1, adj_z)
        grads[3] = lax.dot_general(
            kernel[...], zeta[1], (((0,), (0,)), ((), ())),
            precision=lax.Precision.HIGHEST, preferred_element_type=jnp.float32,
        )
        send_back(1)

    when_owner(compute)
    if stride > 1:
        pl.when(jnp.logical_not(is_owner))(lambda: fetch[7].wait())

    def pass_on(p):
        lo, hi = BACK[p]
        return pltpu.make_async_remote_copy(
            src_ref=ret.at[lo:hi, 0 : work - 1], dst_ref=ret.at[lo:hi, work : 2 * work - 1],
            send_sem=fwd_send.at[p], recv_sem=fwd_recv.at[p],
            device_id=(other, me), device_id_type=MESH,
        )

    for p in range(len(BACK)):
        if stride > 1:
            pl.when(jnp.logical_not(is_owner))(lambda p=p: back_arrive(p, my_slot).wait_recv())

        def taken(d, unused, p=p):
            back_arrive(p, lax.rem(my_slot + d, work)).wait_recv()
            return unused

        lax.fori_loop(1, work, taken, 0)
        when_owner(lambda p=p: back_own(p).wait())
        pass_on(p).start()

    for p in range(len(PHASES) + 1):
        exchange(p).wait_send()
    for p in range(len(PHASES)):

        def gone(d, unused, p=p):
            slot = lax.rem(my_slot + d, work)
            go(p, slot, slot * stride).wait_send()
            return unused

        lax.fori_loop(1, work, gone, 0)
        if stride > 1:
            pl.when(jnp.logical_not(is_owner))(
                lambda p=p: go(p, my_slot, my_slot * stride).wait_send()
            )

    def returned():
        for p in range(len(BACK)):

            def one(d, unused, p=p):
                back(p, lax.rem(me + d, n)).wait_send()
                return unused

            lax.fori_loop(1, n, one, 0)

    when_owner(returned)
    for p in range(len(BACK)):
        pass_on(p).wait()


def place_kernel(work, covered_in, ret_in, switch_in, *refs):
    outs, covered, ret, switch, placed, in_sem, out_sem = refs[:4], *refs[4:]
    blocks, rows_dev, cells = switch.shape
    fetch = [
        pltpu.make_async_copy(covered_in, covered, in_sem.at[0]),
        pltpu.make_async_copy(switch_in, switch, in_sem.at[1]),
    ] + [
        pltpu.make_async_copy(ret_in.at[f], ret.at[f], in_sem.at[2 + f]) for f in range(GRADS)
    ]
    for copy in fetch:
        copy.start()
    fetch[0].wait()
    rank = jnp.int32(0)
    ranks = []
    for b in range(blocks):
        ranks.append(rank)
        rank = rank + covered[0, b]
    many = rank > work
    homes = [
        jnp.where(many, jnp.minimum(r, 2 * work - 2), work - 1) for r in ranks
    ]
    fetch[1].wait()
    for f in range(GRADS):
        fetch[2 + f].wait()
        for b in range(blocks):
            live = jnp.full((rows_dev, cells), covered[0, b]) == 1
            value = ret[f, homes[b]]
            if f == GRADS - 1:
                value = value * jnp.where(switch[b] == 1, PLASTIC, VISCOUS)
            placed[f, b] = jnp.where(live, value, 0.0)
        pltpu.make_async_copy(placed.at[f], outs[f], out_sem.at[f]).start()
    for f in range(GRADS):
        pltpu.make_async_copy(placed.at[f], outs[f], out_sem.at[f]).wait()


def shards(
    velocity, stress, thickness, forcing, switch, covered, reinit, cot_velocity, cot_stress, kernel
):
    blocks, rows_dev, cells = velocity.shape
    n = lax.axis_size("ice")
    work = COVERED // lax.axis_size("ocean")
    rows = kernel.shape[0]
    hbm = pl.BlockSpec(memory_space=pl.ANY)
    i32, f32 = jnp.int32, jnp.float32
    tile = (rows_dev, cells)
    covered = covered.reshape(1, blocks)
    reinit = reinit.reshape(1, blocks)
    operands = (
        velocity, stress, thickness, forcing, switch, cot_velocity, cot_stress, kernel
    )

    ret = pl.pallas_call(
        functools.partial(work_kernel, n, work),
        out_shape=jax.ShapeDtypeStruct((GRADS, 2 * work - 1) + tile, f32),
        in_specs=[hbm] * 10,
        out_specs=hbm,
        scratch_shapes=[pltpu.VMEM(x.shape, x.dtype) for x in operands]
        + [
            pltpu.VMEM((1, blocks), i32),
            pltpu.SMEM((1, blocks), i32),
            pltpu.VMEM((1, cells), i32),
            pltpu.SMEM((1, cells), i32),
            pltpu.VMEM((FIELDS, work) + tile, f32),
            pltpu.VMEM((FIELDS, work - 1) + tile, f32),
            pltpu.VMEM((FIELDS, work - 1) + tile, f32),
            pltpu.VMEM((work,) + tile, f32),
            pltpu.VMEM((work - 1,) + tile, f32),
            pltpu.VMEM((work - 1,) + tile, f32),
            pltpu.VMEM((work, FIELDS) + tile, f32),
            pltpu.VMEM((FIELDS, rows, cells), f32),
            pltpu.VMEM((2, rows, cells), f32),
            pltpu.VMEM((WINDOWS * SUB, rows // SUBLANES, SUBLANES, cells), f32),
            pltpu.VMEM((GRADS, rows, cells), f32),
            pltpu.SemaphoreType.DMA((len(operands),)),
            pltpu.SemaphoreType.DMA((3,)),
            pltpu.SemaphoreType.DMA((len(PHASES) + 1,)),
            pltpu.SemaphoreType.DMA((len(PHASES) + 1,)),
            pltpu.SemaphoreType.DMA((len(PHASES), work)),
            pltpu.SemaphoreType.DMA((len(PHASES), n)),
            pltpu.SemaphoreType.DMA((len(BACK), n)),
            pltpu.SemaphoreType.DMA((len(BACK), work)),
            pltpu.SemaphoreType.DMA((len(BACK),)),
            pltpu.SemaphoreType.DMA((len(BACK),)),
            pltpu.SemaphoreType.DMA((len(BACK),)),
        ],
        compiler_params=pltpu.CompilerParams(
            collective_id=0, has_side_effects=True, vmem_limit_bytes=64 << 20
        ),
    )(covered, reinit, *operands)

    field = jax.ShapeDtypeStruct(velocity.shape, f32)
    grad_u, grad_s, grad_f, grad_q = pl.pallas_call(
        functools.partial(place_kernel, work),
        out_shape=[field] * GRADS,
        in_specs=[hbm] * 3,
        out_specs=[hbm] * GRADS,
        scratch_shapes=[
            pltpu.SMEM((1, blocks), i32),
            pltpu.VMEM(ret.shape, f32),
            pltpu.VMEM(switch.shape, i32),
            pltpu.VMEM((GRADS,) + velocity.shape, f32),
            pltpu.SemaphoreType.DMA((2 + GRADS,)),
            pltpu.SemaphoreType.DMA((GRADS,)),
        ],
        compiler_params=pltpu.CompilerParams(vmem_limit_bytes=64 << 20),
    )(covered, ret, switch)
    return grad_u, grad_s, grad_q, grad_f


def solution(mesh):
    split = P("ocean", "ice", None)
    return jax.shard_map(
        shards,
        mesh=mesh,
        in_specs=(split,) * 5 + (P("ocean"),) * 2 + (split,) * 2 + (P(),),
        out_specs=(split,) * 4,
        check_vma=False,
    )
```

```python
import functools

import jax
import jax.numpy as jnp
from jax import lax
from jax.experimental import pallas as pl
from jax.experimental.pallas import tpu as pltpu
from jax.sharding import PartitionSpec as P

SUB = 8
WINDOWS = 2
COVERED = 32

PLASTIC = 0.25
VISCOUS = 1.0
GAMMA = 0.6
BETA = 0.9
STEP = 0.04

MESH = pl.DeviceIdType.MESH
FIELDS = 6
PHASES = ((0, 1), (1, 3), (3, 6))
GRADS = 4
BACK = ((0, 3), (3, 4))


SUBLANES = 8


def load_tiles(ref, index, rows):
    count = rows // SUBLANES
    return [ref[index, pl.ds(v, SUBLANES, stride=count), :] for v in range(count)]


def store_tiles(ref, index, tiles):
    for v, tile in enumerate(tiles):
        ref[index, pl.ds(v, SUBLANES, stride=len(tiles)), :] = tile


def forward_diff(tiles, row, col):
    first = jnp.where(row == 0, 0.0, pltpu.roll(tiles[-1], 1, 0))
    out = []
    for v, x in enumerate(tiles):
        upper = tiles[v - 1] if v > 0 else first
        left = jnp.where(col == 0, 0.0, pltpu.roll(x, 1, 1))
        out.append((x + x - upper) - left)
    return out


def backward_diff(tiles, row, col):
    last = jnp.where(row == SUBLANES - 1, 0.0, pltpu.roll(tiles[0], SUBLANES - 1, 0))
    cells = tiles[0].shape[1]
    out = []
    for v, x in enumerate(tiles):
        lower = tiles[v + 1] if v + 1 < len(tiles) else last
        right = jnp.where(col == cells - 1, 0.0, pltpu.roll(x, cells - 1, 1))
        out.append((x + x - lower) - right)
    return out


def flips(n):
    far, near = list(range(n // 2, n)), list(range(1, n // 2))
    near.sort(key=lambda x: (x & -x) * n - x, reverse=True)
    return [x for pair in zip(far, near) for x in pair] + far[len(near):]


def flipped(index, bits):
    place = 1
    moved = index
    while place <= bits:
        if bits & place:
            moved = moved + place * (1 - 2 * ((index // place) % 2))
        place *= 2
    return moved


def work_kernel(
    n, work, covered_in, reinit_in, *refs
):
    operands, ret, inputs, (covered, reinit, idx_row, idx), rest = (
        refs[:8], refs[8], refs[9:17], refs[17:21], refs[21:]
    )
    velo, stress, thick, force, switch, cot_u, cot_s, kernel = inputs
    (
        own, over, got, keep_own, keep_over, keep_got, send, arrived, fields, zeta, total, grads, outgoing,
        in_sem, plan_sem, ex_send, ex_recv, go_send, go_recv, back_send, back_recv, own_sem,
        fwd_send, fwd_recv,
    ) = rest
    ocean = lax.axis_index("ocean")
    me = lax.axis_index("ice")
    other = 1 - ocean
    stride = n // work
    rows_dev = velo.shape[1]
    cells = velo.shape[2]
    rows = kernel.shape[0]
    my_slot = me // stride
    is_owner = me % stride == 0

    def when_owner(body):
        if stride == 1:
            body()
        else:
            pl.when(is_owner)(body)

    plan_in = (
        pltpu.make_async_copy(covered_in, covered, plan_sem.at[0]),
        pltpu.make_async_copy(reinit_in, reinit, plan_sem.at[1]),
    )
    fetch = [
        pltpu.make_async_copy(operands[i], inputs[i], in_sem.at[i]) for i in range(len(operands))
    ]
    for copy in plan_in:
        copy.start()
    for i in (2, 4, 5, 6, 0, 1, 3, 7):
        fetch[i].start()

    barrier = pltpu.get_barrier_semaphore()

    def greet(d, unused):
        pl.semaphore_signal(
            barrier, inc=1, device_id=(ocean, lax.rem(me + d, n)), device_id_type=MESH
        )
        return unused

    pl.semaphore_signal(barrier, inc=1, device_id=(other, me), device_id_type=MESH)
    lax.fori_loop(1, n, greet, 0)

    for copy in plan_in:
        copy.wait()
    blocks = covered.shape[1]
    ones = jnp.broadcast_to(covered[...].astype(jnp.float32), (8, blocks))
    upto = (
        lax.broadcasted_iota(jnp.int32, (blocks, blocks), 1)
        <= lax.broadcasted_iota(jnp.int32, (blocks, blocks), 0)
    ).astype(jnp.float32)
    tally = lax.dot_general(
        upto, ones, (((1,), (1,)), ((), ())), preferred_element_type=jnp.float32
    )
    ranks = lax.broadcasted_iota(jnp.int32, (blocks, cells), 1).astype(jnp.float32)
    before = jnp.where(jnp.broadcast_to(tally[:, :1], (blocks, cells)) <= ranks, 1, 0)
    idx_row[...] = jnp.minimum(jnp.sum(before, axis=0, keepdims=True), blocks - 1)
    to_scalars = pltpu.make_async_copy(idx_row, idx, plan_sem.at[2])
    to_scalars.start()
    count = jnp.sum(ones, axis=1, keepdims=True)[:1]
    full = jnp.broadcast_to(count, (rows_dev, cells)) > work + 0.0

    fetched = ((2, 4), (5, 6), (0, 1, 3))
    sources = (None, cot_u, cot_s, velo, stress, force)

    def pack(dst, k, rank, p):
        b = idx[0, rank]
        for f in range(*PHASES[p]):
            if f == 0:
                dst[f, k] = thick[b] * jnp.where(switch[b] == 1, PLASTIC, VISCOUS)
            else:
                dst[f, k] = sources[f][b]

    def pack_keep(dst, k, rank):
        kept = (1 - reinit[0, idx[0, rank]]).astype(jnp.float32)
        dst[k] = jnp.full((rows_dev, cells), kept)

    def exchange(p):
        if p == len(PHASES):
            src, dst = keep_over, keep_got
        else:
            lo, hi = PHASES[p]
            src, dst = over.at[lo:hi], got.at[lo:hi]
        return pltpu.make_async_remote_copy(
            src_ref=src, dst_ref=dst, send_sem=ex_send.at[p], recv_sem=ex_recv.at[p],
            device_id=(other, me), device_id_type=MESH,
        )

    to_scalars.wait()

    def pack_phase(p):
        for i in fetched[p]:
            fetch[i].wait()
        for k in range(work - 1):
            pack(over, k, work + k, p)
        if p == 0:
            pl.semaphore_wait(barrier, n)
        exchange(p).start()
        for k in range(work):
            pack(own, k, k, p)

    def pack_keeps():
        for k in range(work - 1):
            pack_keep(keep_over, k, work + k)
        exchange(len(PHASES)).start()
        for k in range(work):
            pack_keep(keep_own, k, k)


    def go(p, slot, target):
        lo, hi = PHASES[p]
        return pltpu.make_async_remote_copy(
            src_ref=send.at[slot, lo:hi], dst_ref=arrived.at[me, lo:hi],
            send_sem=go_send.at[p, slot], recv_sem=go_recv.at[p, me],
            device_id=(ocean, target), device_id_type=MESH,
        )

    def arrive(p, j):
        lo, hi = PHASES[p]
        return pltpu.make_async_remote_copy(
            src_ref=send.at[0, lo:hi], dst_ref=arrived.at[j, lo:hi],
            send_sem=go_send.at[p, 0], recv_sem=go_recv.at[p, j],
            device_id=(ocean, j), device_id_type=MESH,
        )

    pack_phase(0)
    pack_phase(1)
    for p, (lo, hi) in enumerate(PHASES):
        exchange(p).wait_recv()
        for k in range(work):
            for f in range(lo, hi):
                rest = got[f, k] if k < work - 1 else own[f, 0]
                send[k, f] = jnp.where(full, own[f, k], rest)

        for bits in flips(work):
            slot = flipped(my_slot, bits)
            go(p, slot, slot * stride).start()

        def local(lo=lo, hi=hi):
            arrived[me, lo:hi] = send[my_slot, lo:hi]

        when_owner(local)
        if stride > 1:
            pl.when(jnp.logical_not(is_owner))(lambda p=p: go(p, my_slot, my_slot * stride).start())
        if p == 0:
            pack_phase(2)
        elif p == 1:
            pack_keeps()
    exchange(len(PHASES)).wait_recv()

    def wait_phase(p):
        def one(d, unused):
            arrive(p, lax.rem(me + n - d, n)).wait_recv()
            return unused

        lax.fori_loop(1, n, one, 0)
        for f in range(*PHASES[p]):
            for j in range(n):
                fields[f, j * rows_dev : (j + 1) * rows_dev, :] = arrived[j, f]

    def back(p, j):
        lo, hi = BACK[p]
        return pltpu.make_async_remote_copy(
            src_ref=outgoing.at[j, lo:hi], dst_ref=ret.at[my_slot, lo:hi],
            send_sem=back_send.at[p, j], recv_sem=back_recv.at[p, my_slot],
            device_id=(ocean, j), device_id_type=MESH,
        )

    def back_own(p):
        lo, hi = BACK[p]
        return pltpu.make_async_copy(
            outgoing.at[me, lo:hi], ret.at[my_slot, lo:hi], own_sem.at[p]
        )

    def back_arrive(p, slot):
        lo, hi = BACK[p]
        return pltpu.make_async_remote_copy(
            src_ref=outgoing.at[0, lo:hi], dst_ref=ret.at[slot, lo:hi],
            send_sem=back_send.at[p, 0], recv_sem=back_recv.at[p, slot],
            device_id=(ocean, slot * stride), device_id_type=MESH,
        )

    def send_back(p):
        lo, hi = BACK[p]

        for f in range(lo, hi):
            for j in range(n):
                outgoing[j, f] = grads[f, j * rows_dev : (j + 1) * rows_dev, :]
        for bits in flips(n):
            back(p, flipped(me, bits)).start()
        back_own(p).start()

    def compute():
        row = lax.broadcasted_iota(jnp.int32, (SUBLANES, cells), 0)
        col = lax.broadcasted_iota(jnp.int32, (SUBLANES, cells), 1)
        got_slot = jnp.minimum(my_slot, work - 2)
        spare = jnp.where(
            jnp.full((rows_dev, cells), my_slot) < work - 1, keep_got[got_slot], keep_own[0]
        )
        scale = jnp.where(full, keep_own[my_slot], spare)[:1]
        scale = jnp.broadcast_to(scale, (SUBLANES, cells))
        fetch[7].wait()
        wait_phase(0)
        zeta[0] = -STEP * jnp.dot(
            kernel[...], fields[0], precision=lax.Precision.HIGHEST,
            preferred_element_type=jnp.float32,
        )
        wait_phase(1)
        tiles = range(rows // SUBLANES)
        blank = jnp.zeros((SUBLANES, cells), jnp.float32)
        scaled = load_tiles(zeta, 0, rows)

        adj = [-STEP * x for x in load_tiles(fields, 1, rows)]
        adj_s = load_tiles(fields, 2, rows)
        adj_f = [blank for v in tiles]
        for step in range(WINDOWS * SUB - 1, -1, -1):
            diff = forward_diff(adj, row, col)
            total_s = [adj_s[v] + diff[v] for v in tiles]
            for v in tiles:
                total[step, v] = total_s[v]
            adj_f = [adj_f[v] + adj[v] for v in tiles]
            diff = backward_diff([scaled[v] * total_s[v] for v in tiles], row, col)
            adj = [BETA * adj[v] + diff[v] for v in tiles]
            adj_s = [GAMMA * total_s[v] for v in tiles]
            if step > 0 and step % SUB == 0:
                adj_s = [x * scale for x in adj_s]
        store_tiles(grads, 0, [x * (-1.0 / STEP) for x in adj])
        store_tiles(grads, 1, adj_s)
        store_tiles(grads, 2, [-x for x in adj_f])
        send_back(0)
        wait_phase(2)

        u_now = load_tiles(fields, 3, rows)
        r_now = [-STEP * x for x in load_tiles(fields, 4, rows)]
        pushed = [STEP * x for x in load_tiles(fields, 5, rows)]
        scaled = load_tiles(zeta, 0, rows)
        adj_z = [blank for v in tiles]
        for step in range(WINDOWS * SUB):
            if step > 0 and step % SUB == 0:
                r_now = [x * scale for x in r_now]
            strain = forward_diff(u_now, row, col)
            adj_z = [adj_z[v] + total[step, v] * strain[v] for v in tiles]
            r_now = [GAMMA * r_now[v] + scaled[v] * strain[v] for v in tiles]
            if step < WINDOWS * SUB - 1:
                diff = backward_diff(r_now, row, col)
                u_now = [BETA * u_now[v] + diff[v] + pushed[v] for v in tiles]
        store_tiles(zeta, 1, adj_z)
        grads[3] = lax.dot_general(
            kernel[...], zeta[1], (((0,), (0,)), ((), ())),
            precision=lax.Precision.HIGHEST, preferred_element_type=jnp.float32,
        )
        send_back(1)

    when_owner(compute)
    if stride > 1:
        pl.when(jnp.logical_not(is_owner))(lambda: fetch[7].wait())

    def pass_on(p):
        lo, hi = BACK[p]
        return pltpu.make_async_remote_copy(
            src_ref=ret.at[0 : work - 1, lo:hi], dst_ref=ret.at[work : 2 * work - 1, lo:hi],
            send_sem=fwd_send.at[p], recv_sem=fwd_recv.at[p],
            device_id=(other, me), device_id_type=MESH,
        )

    for p in range(len(BACK)):
        if stride > 1:
            pl.when(jnp.logical_not(is_owner))(lambda p=p: back_arrive(p, my_slot).wait_recv())

        def taken(d, unused, p=p):
            back_arrive(p, lax.rem(my_slot + d, work)).wait_recv()
            return unused

        lax.fori_loop(1, work, taken, 0)
        when_owner(lambda p=p: back_own(p).wait())
        pass_on(p).start()

    for p in range(len(PHASES) + 1):
        exchange(p).wait_send()
    for p in range(len(PHASES)):

        def gone(d, unused, p=p):
            slot = lax.rem(my_slot + d, work)
            go(p, slot, slot * stride).wait_send()
            return unused

        lax.fori_loop(1, work, gone, 0)
        if stride > 1:
            pl.when(jnp.logical_not(is_owner))(
                lambda p=p: go(p, my_slot, my_slot * stride).wait_send()
            )

    def returned():
        for p in range(len(BACK)):

            def one(d, unused, p=p):
                back(p, lax.rem(me + d, n)).wait_send()
                return unused

            lax.fori_loop(1, n, one, 0)

    when_owner(returned)
    for p in range(len(BACK)):
        pass_on(p).wait()


def place_kernel(work, covered_in, ret_in, switch_in, *refs):
    outs, covered, ret, switch, placed, in_sem, out_sem = refs[:4], *refs[4:]
    blocks, rows_dev, cells = switch.shape
    fetch = [
        pltpu.make_async_copy(covered_in, covered, in_sem.at[0]),
        pltpu.make_async_copy(switch_in, switch, in_sem.at[1]),
        pltpu.make_async_copy(ret_in, ret, in_sem.at[2]),
    ]
    for copy in fetch:
        copy.start()
    fetch[0].wait()
    rank = jnp.int32(0)
    ranks = []
    for b in range(blocks):
        ranks.append(rank)
        rank = rank + covered[0, b]
    many = rank > work
    homes = [
        jnp.where(many, jnp.minimum(r, 2 * work - 2), work - 1) for r in ranks
    ]
    fetch[1].wait()
    fetch[2].wait()
    for f in range(GRADS):
        for b in range(blocks):
            live = jnp.full((rows_dev, cells), covered[0, b]) == 1
            value = ret[homes[b], f]
            if f == GRADS - 1:
                value = value * jnp.where(switch[b] == 1, PLASTIC, VISCOUS)
            placed[f, b] = jnp.where(live, value, 0.0)
        pltpu.make_async_copy(placed.at[f], outs[f], out_sem.at[f]).start()
    for f in range(GRADS):
        pltpu.make_async_copy(placed.at[f], outs[f], out_sem.at[f]).wait()


def shards(
    velocity, stress, thickness, forcing, switch, covered, reinit, cot_velocity, cot_stress, kernel
):
    blocks, rows_dev, cells = velocity.shape
    n = lax.axis_size("ice")
    work = COVERED // lax.axis_size("ocean")
    rows = kernel.shape[0]
    hbm = pl.BlockSpec(memory_space=pl.ANY)
    i32, f32 = jnp.int32, jnp.float32
    tile = (rows_dev, cells)
    covered = covered.reshape(1, blocks)
    reinit = reinit.reshape(1, blocks)
    operands = (
        velocity, stress, thickness, forcing, switch, cot_velocity, cot_stress, kernel
    )

    ret = pl.pallas_call(
        functools.partial(work_kernel, n, work),
        out_shape=jax.ShapeDtypeStruct((2 * work - 1, GRADS) + tile, f32),
        in_specs=[hbm] * 10,
        out_specs=hbm,
        scratch_shapes=[pltpu.VMEM(x.shape, x.dtype) for x in operands]
        + [
            pltpu.VMEM((1, blocks), i32),
            pltpu.SMEM((1, blocks), i32),
            pltpu.VMEM((1, cells), i32),
            pltpu.SMEM((1, cells), i32),
            pltpu.VMEM((FIELDS, work) + tile, f32),
            pltpu.VMEM((FIELDS, work - 1) + tile, f32),
            pltpu.VMEM((FIELDS, work - 1) + tile, f32),
            pltpu.VMEM((work,) + tile, f32),
            pltpu.VMEM((work - 1,) + tile, f32),
            pltpu.VMEM((work - 1,) + tile, f32),
            pltpu.VMEM((work, FIELDS) + tile, f32),
            pltpu.VMEM((n, FIELDS) + tile, f32),
            pltpu.VMEM((FIELDS, rows, cells), f32),
            pltpu.VMEM((2, rows, cells), f32),
            pltpu.VMEM((WINDOWS * SUB, rows // SUBLANES, SUBLANES, cells), f32),
            pltpu.VMEM((GRADS, rows, cells), f32),
            pltpu.VMEM((n, GRADS) + tile, f32),
            pltpu.SemaphoreType.DMA((len(operands),)),
            pltpu.SemaphoreType.DMA((3,)),
            pltpu.SemaphoreType.DMA((len(PHASES) + 1,)),
            pltpu.SemaphoreType.DMA((len(PHASES) + 1,)),
            pltpu.SemaphoreType.DMA((len(PHASES), work)),
            pltpu.SemaphoreType.DMA((len(PHASES), n)),
            pltpu.SemaphoreType.DMA((len(BACK), n)),
            pltpu.SemaphoreType.DMA((len(BACK), work)),
            pltpu.SemaphoreType.DMA((len(BACK),)),
            pltpu.SemaphoreType.DMA((len(BACK),)),
            pltpu.SemaphoreType.DMA((len(BACK),)),
        ],
        compiler_params=pltpu.CompilerParams(
            collective_id=0, has_side_effects=True, vmem_limit_bytes=64 << 20
        ),
    )(covered, reinit, *operands)

    field = jax.ShapeDtypeStruct(velocity.shape, f32)
    grad_u, grad_s, grad_f, grad_q = pl.pallas_call(
        functools.partial(place_kernel, work),
        out_shape=[field] * GRADS,
        in_specs=[hbm] * 3,
        out_specs=[hbm] * GRADS,
        scratch_shapes=[
            pltpu.SMEM((1, blocks), i32),
            pltpu.VMEM(ret.shape, f32),
            pltpu.VMEM(switch.shape, i32),
            pltpu.VMEM((GRADS,) + velocity.shape, f32),
            pltpu.SemaphoreType.DMA((3,)),
            pltpu.SemaphoreType.DMA((GRADS,)),
        ],
        compiler_params=pltpu.CompilerParams(vmem_limit_bytes=64 << 20),
    )(covered, ret, switch)
    return grad_u, grad_s, grad_q, grad_f


def solution(mesh):
    split = P("ocean", "ice", None)
    return jax.shard_map(
        shards,
        mesh=mesh,
        in_specs=(split,) * 5 + (P("ocean"),) * 2 + (split,) * 2 + (P(),),
        out_specs=(split,) * 4,
        check_vma=False,
    )
```

```python
import functools

import jax
import jax.numpy as jnp
from jax import lax
from jax.experimental import pallas as pl
from jax.experimental.pallas import tpu as pltpu
from jax.sharding import PartitionSpec as P

SUB = 8
WINDOWS = 2
COVERED = 32

PLASTIC = 0.25
VISCOUS = 1.0
GAMMA = 0.6
BETA = 0.9
STEP = 0.04

MESH = pl.DeviceIdType.MESH
FIELDS = 6
PHASES = ((0, 1), (1, 3), (3, 6))
GRADS = 4
BACK = ((0, 3), (3, 4))
PARTS = 4


SUBLANES = 8


def load_tiles(ref, index, rows):
    count = rows // SUBLANES
    return [ref[index, pl.ds(v, SUBLANES, stride=count), :] for v in range(count)]


def store_tiles(ref, index, tiles):
    for v, tile in enumerate(tiles):
        ref[index, pl.ds(v, SUBLANES, stride=len(tiles)), :] = tile


def forward_diff(tiles, row, col):
    first = jnp.where(row == 0, 0.0, pltpu.roll(tiles[-1], 1, 0))
    out = []
    for v, x in enumerate(tiles):
        upper = tiles[v - 1] if v > 0 else first
        left = jnp.where(col == 0, 0.0, pltpu.roll(x, 1, 1))
        out.append((x + x - upper) - left)
    return out


def backward_diff(tiles, row, col):
    last = jnp.where(row == SUBLANES - 1, 0.0, pltpu.roll(tiles[0], SUBLANES - 1, 0))
    cells = tiles[0].shape[1]
    out = []
    for v, x in enumerate(tiles):
        lower = tiles[v + 1] if v + 1 < len(tiles) else last
        right = jnp.where(col == cells - 1, 0.0, pltpu.roll(x, cells - 1, 1))
        out.append((x + x - lower) - right)
    return out


def flips(n):
    far, near = list(range(n // 2, n)), list(range(1, n // 2))
    near.sort(key=lambda x: (x & -x) * n - x, reverse=True)
    return [x for pair in zip(far, near) for x in pair] + far[len(near):]


def flipped(index, bits):
    place = 1
    moved = index
    while place <= bits:
        if bits & place:
            moved = moved + place * (1 - 2 * ((index // place) % 2))
        place *= 2
    return moved


def work_kernel(
    n, work, covered_in, reinit_in, *refs
):
    operands, ret, inputs, (covered, reinit, idx_row, idx), rest = (
        refs[:8], refs[8], refs[9:17], refs[17:21], refs[21:]
    )
    velo, stress, thick, force, switch, cot_u, cot_s, kernel = inputs
    (
        own, over, got, keep_own, keep_over, keep_got, send, arrived, fields, zeta, total, grads, outgoing, landed,
        in_sem, plan_sem, ex_send, ex_recv, go_send, go_recv, back_send, back_recv, own_sem,
        fwd_send, fwd_recv,
    ) = rest
    ocean = lax.axis_index("ocean")
    me = lax.axis_index("ice")
    other = 1 - ocean
    stride = n // work
    rows_dev = velo.shape[1]
    cells = velo.shape[2]
    rows = kernel.shape[0]
    my_slot = me // stride
    is_owner = me % stride == 0

    def when_owner(body):
        if stride == 1:
            body()
        else:
            pl.when(is_owner)(body)

    plan_in = (
        pltpu.make_async_copy(covered_in, covered, plan_sem.at[0]),
        pltpu.make_async_copy(reinit_in, reinit, plan_sem.at[1]),
    )
    fetch = [
        pltpu.make_async_copy(operands[i], inputs[i], in_sem.at[i]) for i in range(len(operands))
    ]
    for copy in plan_in:
        copy.start()
    for i in (2, 4, 5, 6, 0, 1, 3, 7):
        fetch[i].start()

    barrier = pltpu.get_barrier_semaphore()

    def greet(d, unused):
        pl.semaphore_signal(
            barrier, inc=1, device_id=(ocean, lax.rem(me + d, n)), device_id_type=MESH
        )
        return unused

    pl.semaphore_signal(barrier, inc=1, device_id=(other, me), device_id_type=MESH)
    lax.fori_loop(1, n, greet, 0)

    for copy in plan_in:
        copy.wait()
    blocks = covered.shape[1]
    ones = jnp.broadcast_to(covered[...].astype(jnp.float32), (8, blocks))
    upto = (
        lax.broadcasted_iota(jnp.int32, (blocks, blocks), 1)
        <= lax.broadcasted_iota(jnp.int32, (blocks, blocks), 0)
    ).astype(jnp.float32)
    tally = lax.dot_general(
        upto, ones, (((1,), (1,)), ((), ())), preferred_element_type=jnp.float32
    )
    ranks = lax.broadcasted_iota(jnp.int32, (blocks, cells), 1).astype(jnp.float32)
    before = jnp.where(jnp.broadcast_to(tally[:, :1], (blocks, cells)) <= ranks, 1, 0)
    idx_row[...] = jnp.minimum(jnp.sum(before, axis=0, keepdims=True), blocks - 1)
    to_scalars = pltpu.make_async_copy(idx_row, idx, plan_sem.at[2])
    to_scalars.start()
    count = jnp.sum(ones, axis=1, keepdims=True)[:1]
    full = jnp.broadcast_to(count, (rows_dev, cells)) > work + 0.0

    fetched = ((2, 4), (5, 6), (0, 1, 3))
    sources = (None, cot_u, cot_s, velo, stress, force)

    def pack(dst, k, rank, p):
        b = idx[0, rank]
        for f in range(*PHASES[p]):
            if f == 0:
                dst[f, k] = thick[b] * jnp.where(switch[b] == 1, PLASTIC, VISCOUS)
            else:
                dst[f, k] = sources[f][b]

    def pack_keep(dst, k, rank):
        kept = (1 - reinit[0, idx[0, rank]]).astype(jnp.float32)
        dst[k] = jnp.full((rows_dev, cells), kept)

    def exchange(p):
        if p == len(PHASES):
            src, dst = keep_over, keep_got
        else:
            lo, hi = PHASES[p]
            src, dst = over.at[lo:hi], got.at[lo:hi]
        return pltpu.make_async_remote_copy(
            src_ref=src, dst_ref=dst, send_sem=ex_send.at[p], recv_sem=ex_recv.at[p],
            device_id=(other, me), device_id_type=MESH,
        )

    to_scalars.wait()

    def pack_phase(p):
        for i in fetched[p]:
            fetch[i].wait()
        for k in range(work - 1):
            pack(over, k, work + k, p)
        if p == 0:
            pl.semaphore_wait(barrier, n)
        exchange(p).start()
        for k in range(work):
            pack(own, k, k, p)

    def pack_keeps():
        for k in range(work - 1):
            pack_keep(keep_over, k, work + k)
        exchange(len(PHASES)).start()
        for k in range(work):
            pack_keep(keep_own, k, k)


    def go(p, slot, target):
        lo, hi = PHASES[p]
        return pltpu.make_async_remote_copy(
            src_ref=send.at[slot, lo:hi], dst_ref=arrived.at[me, lo:hi],
            send_sem=go_send.at[p, slot], recv_sem=go_recv.at[p, me],
            device_id=(ocean, target), device_id_type=MESH,
        )

    def arrive(p, j):
        lo, hi = PHASES[p]
        return pltpu.make_async_remote_copy(
            src_ref=send.at[0, lo:hi], dst_ref=arrived.at[j, lo:hi],
            send_sem=go_send.at[p, 0], recv_sem=go_recv.at[p, j],
            device_id=(ocean, j), device_id_type=MESH,
        )

    pack_phase(0)
    pack_phase(1)
    for p, (lo, hi) in enumerate(PHASES):
        exchange(p).wait_recv()
        for k in range(work):
            for f in range(lo, hi):
                rest = got[f, k] if k < work - 1 else own[f, 0]
                send[k, f] = jnp.where(full, own[f, k], rest)

        for bits in flips(work):
            slot = flipped(my_slot, bits)
            go(p, slot, slot * stride).start()

        def local(lo=lo, hi=hi):
            arrived[me, lo:hi] = send[my_slot, lo:hi]

        when_owner(local)
        if stride > 1:
            pl.when(jnp.logical_not(is_owner))(lambda p=p: go(p, my_slot, my_slot * stride).start())
        if p == 0:
            pack_phase(2)
        elif p == 1:
            pack_keeps()
    exchange(len(PHASES)).wait_recv()

    def wait_phase(p):
        def one(d, unused):
            arrive(p, lax.rem(me + n - d, n)).wait_recv()
            return unused

        lax.fori_loop(1, n, one, 0)
        for f in range(*PHASES[p]):
            for j in range(n):
                fields[f, j * rows_dev : (j + 1) * rows_dev, :] = arrived[j, f]

    def back(p, j):
        lo, hi = BACK[p]
        return pltpu.make_async_remote_copy(
            src_ref=outgoing.at[j, lo:hi], dst_ref=landed.at[my_slot, lo:hi],
            send_sem=back_send.at[p, j], recv_sem=back_recv.at[p, my_slot],
            device_id=(ocean, j), device_id_type=MESH,
        )

    def keep_own_part(p):
        lo, hi = BACK[p]
        return pltpu.make_async_copy(
            landed.at[:, lo:hi], ret.at[0:work, lo:hi], own_sem.at[p]
        )

    def back_arrive(p, slot):
        lo, hi = BACK[p]
        return pltpu.make_async_remote_copy(
            src_ref=outgoing.at[0, lo:hi], dst_ref=landed.at[slot, lo:hi],
            send_sem=back_send.at[p, 0], recv_sem=back_recv.at[p, slot],
            device_id=(ocean, slot * stride), device_id_type=MESH,
        )

    def send_back(p):
        lo, hi = BACK[p]

        for f in range(lo, hi):
            for j in range(n):
                outgoing[j, f] = grads[f, j * rows_dev : (j + 1) * rows_dev, :]
        for bits in flips(n):
            back(p, flipped(me, bits)).start()
        landed[my_slot, lo:hi] = outgoing[me, lo:hi]

    def compute():
        row = lax.broadcasted_iota(jnp.int32, (SUBLANES, cells), 0)
        col = lax.broadcasted_iota(jnp.int32, (SUBLANES, cells), 1)
        got_slot = jnp.minimum(my_slot, work - 2)
        spare = jnp.where(
            jnp.full((rows_dev, cells), my_slot) < work - 1, keep_got[got_slot], keep_own[0]
        )
        scale = jnp.where(full, keep_own[my_slot], spare)[:1]
        scale = jnp.broadcast_to(scale, (SUBLANES, cells))
        fetch[7].wait()
        wait_phase(0)
        zeta[0] = -STEP * jnp.dot(
            kernel[...], fields[0], precision=lax.Precision.HIGHEST,
            preferred_element_type=jnp.float32,
        )
        wait_phase(1)
        tiles = range(rows // SUBLANES)
        blank = jnp.zeros((SUBLANES, cells), jnp.float32)
        scaled = load_tiles(zeta, 0, rows)

        adj = [-STEP * x for x in load_tiles(fields, 1, rows)]
        adj_s = load_tiles(fields, 2, rows)
        adj_f = [blank for v in tiles]
        for step in range(WINDOWS * SUB - 1, -1, -1):
            diff = forward_diff(adj, row, col)
            total_s = [adj_s[v] + diff[v] for v in tiles]
            for v in tiles:
                total[step, v] = total_s[v]
            adj_f = [adj_f[v] + adj[v] for v in tiles]
            diff = backward_diff([scaled[v] * total_s[v] for v in tiles], row, col)
            adj = [BETA * adj[v] + diff[v] for v in tiles]
            adj_s = [GAMMA * total_s[v] for v in tiles]
            if step > 0 and step % SUB == 0:
                adj_s = [x * scale for x in adj_s]
        store_tiles(grads, 0, [x * (-1.0 / STEP) for x in adj])
        store_tiles(grads, 1, adj_s)
        store_tiles(grads, 2, [-x for x in adj_f])
        send_back(0)
        wait_phase(2)

        u_now = load_tiles(fields, 3, rows)
        r_now = [-STEP * x for x in load_tiles(fields, 4, rows)]
        pushed = [STEP * x for x in load_tiles(fields, 5, rows)]
        scaled = load_tiles(zeta, 0, rows)
        adj_z = [blank for v in tiles]
        for step in range(WINDOWS * SUB):
            if step > 0 and step % SUB == 0:
                r_now = [x * scale for x in r_now]
            strain = forward_diff(u_now, row, col)
            adj_z = [adj_z[v] + total[step, v] * strain[v] for v in tiles]
            r_now = [GAMMA * r_now[v] + scaled[v] * strain[v] for v in tiles]
            if step < WINDOWS * SUB - 1:
                diff = backward_diff(r_now, row, col)
                u_now = [BETA * u_now[v] + diff[v] + pushed[v] for v in tiles]
        store_tiles(zeta, 1, adj_z)
        grads[3] = lax.dot_general(
            kernel[...], zeta[1], (((0,), (0,)), ((), ())),
            precision=lax.Precision.HIGHEST, preferred_element_type=jnp.float32,
        )
        send_back(1)

    when_owner(compute)
    if stride > 1:
        pl.when(jnp.logical_not(is_owner))(lambda: fetch[7].wait())

    def pass_on(p):
        lo, hi = BACK[p]
        return pltpu.make_async_remote_copy(
            src_ref=landed.at[0 : work - 1, lo:hi], dst_ref=ret.at[work : 2 * work - 1, lo:hi],
            send_sem=fwd_send.at[p], recv_sem=fwd_recv.at[p],
            device_id=(other, me), device_id_type=MESH,
        )

    for p in range(len(BACK)):
        if stride > 1:
            pl.when(jnp.logical_not(is_owner))(lambda p=p: back_arrive(p, my_slot).wait_recv())

        def taken(d, unused, p=p):
            back_arrive(p, lax.rem(my_slot + d, work)).wait_recv()
            return unused

        lax.fori_loop(1, work, taken, 0)
        pass_on(p).start()
        keep_own_part(p).start()

    for p in range(len(PHASES) + 1):
        exchange(p).wait_send()
    for p in range(len(PHASES)):

        def gone(d, unused, p=p):
            slot = lax.rem(my_slot + d, work)
            go(p, slot, slot * stride).wait_send()
            return unused

        lax.fori_loop(1, work, gone, 0)
        if stride > 1:
            pl.when(jnp.logical_not(is_owner))(
                lambda p=p: go(p, my_slot, my_slot * stride).wait_send()
            )

    def returned():
        for p in range(len(BACK)):

            def one(d, unused, p=p):
                back(p, lax.rem(me + d, n)).wait_send()
                return unused

            lax.fori_loop(1, n, one, 0)

    when_owner(returned)
    for p in range(len(BACK)):
        pass_on(p).wait()
        keep_own_part(p).wait()


def place_kernel(work, covered_in, ret_in, switch_in, *refs):
    outs, covered, ret, switch, placed, in_sem, out_sem = refs[:4], *refs[4:]
    blocks, rows_dev, cells = switch.shape
    fetch = [
        pltpu.make_async_copy(covered_in, covered, in_sem.at[0]),
        pltpu.make_async_copy(switch_in, switch, in_sem.at[1]),
        pltpu.make_async_copy(ret_in, ret, in_sem.at[2]),
    ]
    for copy in fetch:
        copy.start()
    fetch[0].wait()
    rank = jnp.int32(0)
    ranks = []
    for b in range(blocks):
        ranks.append(rank)
        rank = rank + covered[0, b]
    many = rank > work
    homes = [
        jnp.where(many, jnp.minimum(r, 2 * work - 2), work - 1) for r in ranks
    ]
    fetch[1].wait()
    fetch[2].wait()
    part = blocks // PARTS
    sent = []
    for b in range(blocks):
        live = jnp.full((rows_dev, cells), covered[0, b]) == 1
        home = homes[b]
        for f in range(GRADS):
            value = ret[home, f]
            if f == GRADS - 1:
                value = value * jnp.where(switch[b] == 1, PLASTIC, VISCOUS)
            placed[f, b] = jnp.where(live, value, 0.0)
        if (b + 1) % part == 0:
            for f in range(GRADS):
                span = pl.ds(b + 1 - part, part)
                copy = pltpu.make_async_copy(
                    placed.at[f, span], outs[f].at[span], out_sem.at[f, b // part]
                )
                copy.start()
                sent.append(copy)
    for copy in sent:
        copy.wait()


def shards(
    velocity, stress, thickness, forcing, switch, covered, reinit, cot_velocity, cot_stress, kernel
):
    blocks, rows_dev, cells = velocity.shape
    n = lax.axis_size("ice")
    work = COVERED // lax.axis_size("ocean")
    rows = kernel.shape[0]
    hbm = pl.BlockSpec(memory_space=pl.ANY)
    i32, f32 = jnp.int32, jnp.float32
    tile = (rows_dev, cells)
    covered = covered.reshape(1, blocks)
    reinit = reinit.reshape(1, blocks)
    operands = (
        velocity, stress, thickness, forcing, switch, cot_velocity, cot_stress, kernel
    )

    ret = pl.pallas_call(
        functools.partial(work_kernel, n, work),
        out_shape=jax.ShapeDtypeStruct((2 * work - 1, GRADS) + tile, f32),
        in_specs=[hbm] * 10,
        out_specs=hbm,
        scratch_shapes=[pltpu.VMEM(x.shape, x.dtype) for x in operands]
        + [
            pltpu.VMEM((1, blocks), i32),
            pltpu.SMEM((1, blocks), i32),
            pltpu.VMEM((1, cells), i32),
            pltpu.SMEM((1, cells), i32),
            pltpu.VMEM((FIELDS, work) + tile, f32),
            pltpu.VMEM((FIELDS, work - 1) + tile, f32),
            pltpu.VMEM((FIELDS, work - 1) + tile, f32),
            pltpu.VMEM((work,) + tile, f32),
            pltpu.VMEM((work - 1,) + tile, f32),
            pltpu.VMEM((work - 1,) + tile, f32),
            pltpu.VMEM((work, FIELDS) + tile, f32),
            pltpu.VMEM((n, FIELDS) + tile, f32),
            pltpu.VMEM((FIELDS, rows, cells), f32),
            pltpu.VMEM((2, rows, cells), f32),
            pltpu.VMEM((WINDOWS * SUB, rows // SUBLANES, SUBLANES, cells), f32),
            pltpu.VMEM((GRADS, rows, cells), f32),
            pltpu.VMEM((n, GRADS) + tile, f32),
            pltpu.VMEM((work, GRADS) + tile, f32),
            pltpu.SemaphoreType.DMA((len(operands),)),
            pltpu.SemaphoreType.DMA((3,)),
            pltpu.SemaphoreType.DMA((len(PHASES) + 1,)),
            pltpu.SemaphoreType.DMA((len(PHASES) + 1,)),
            pltpu.SemaphoreType.DMA((len(PHASES), work)),
            pltpu.SemaphoreType.DMA((len(PHASES), n)),
            pltpu.SemaphoreType.DMA((len(BACK), n)),
            pltpu.SemaphoreType.DMA((len(BACK), work)),
            pltpu.SemaphoreType.DMA((len(BACK),)),
            pltpu.SemaphoreType.DMA((len(BACK),)),
            pltpu.SemaphoreType.DMA((len(BACK),)),
        ],
        compiler_params=pltpu.CompilerParams(
            collective_id=0, has_side_effects=True, vmem_limit_bytes=64 << 20
        ),
    )(covered, reinit, *operands)

    field = jax.ShapeDtypeStruct(velocity.shape, f32)
    grad_u, grad_s, grad_f, grad_q = pl.pallas_call(
        functools.partial(place_kernel, work),
        out_shape=[field] * GRADS,
        in_specs=[hbm] * 3,
        out_specs=[hbm] * GRADS,
        scratch_shapes=[
            pltpu.SMEM((1, blocks), i32),
            pltpu.VMEM(ret.shape, f32),
            pltpu.VMEM(switch.shape, i32),
            pltpu.VMEM((GRADS,) + velocity.shape, f32),
            pltpu.SemaphoreType.DMA((3,)),
            pltpu.SemaphoreType.DMA((GRADS, PARTS)),
        ],
        compiler_params=pltpu.CompilerParams(vmem_limit_bytes=64 << 20),
    )(covered, ret, switch)
    return grad_u, grad_s, grad_q, grad_f


def solution(mesh):
    split = P("ocean", "ice", None)
    return jax.shard_map(
        shards,
        mesh=mesh,
        in_specs=(split,) * 5 + (P("ocean"),) * 2 + (split,) * 2 + (P(),),
        out_specs=(split,) * 4,
        check_vma=False,
    )
```
